128 devices in a mesh: ctx: 32 (over z, y, core), head: 4 (over x).
Axes of the slice: x: 4, y: 4, z: 4, core: 2. Of those that a mesh axis runs over, the one named last changes fastest.
Arguments:
- queries: bfloat16 [4096, 4096], P(('ctx', 'head')), may hold values from -7.2 to 7.2
- keys: bfloat16 [4096, 512], P(('ctx', 'head')), may hold values from -7.2 to 7.2
- values: bfloat16 [4096, 512], P(('ctx', 'head')), may hold values from -6 to 6
- grad_out: bfloat16 [4096, 4096], P('ctx', 'head'), may hold values from -6 to 6
- owner_lists: int32 [32, 2], replicated, may hold values from 0 to 63, as said below
- doc_lengths: int32 [16], replicated, may hold values from 1 to 2048, as said below
Outputs:
- attn_out: bfloat16 [4096, 4096], P('ctx', 'head')
- grad_q: bfloat16 [4096, 4096], P(('ctx', 'head'))
- grad_k: bfloat16 [4096, 512], P(('ctx', 'head'))
- grad_v: bfloat16 [4096, 512], P(('ctx', 'head'))
The draws below stay inside these ranges and needn't reach their ends.
Inputs may be any that keep to these rules, and one draw needn't show every extreme that they name: `owner_lists`: row r names the two stretches of 64 positions that owner r receives; each of the 64 stretches is named exactly once. `doc_lengths`: lengths of the packed documents in order; they sum to 4096 and the longest is exactly 2048.
All inputs are finite; a program needn't handle non-finite values.
Results may differ from the reference program's by a relative error of at most 0.015.
Values may be sent and summed in bfloat16 or wider, within the bound.
A program may use at most 64 MiB of HBM per device.

```python
import math
import jax
import jax.numpy as jnp
from jax import lax

HEAD_DIM = 128
GROUP = 8
KV_HEADS = 4
Q_HEADS = 32
TOK_DEV = 128
NDOCS = 16
SEQ = 4096
STRETCH = 64
DOC_MOST = 2048
N_CTX = 32


def doc_plan(key):
    remaining = SEQ - DOC_MOST
    pieces_cut = jnp.sort(jax.random.permutation(jax.random.fold_in(key, 21), remaining - 1)[:NDOCS - 2] + 1)
    borders = jnp.concatenate([jnp.zeros((1,), jnp.int32), pieces_cut.astype(jnp.int32), jnp.full((1,), remaining, jnp.int32)])
    smaller = borders[1:] - borders[:-1]
    big_spot = jax.random.randint(jax.random.fold_in(key, 22), (), 0, NDOCS)
    places = jnp.arange(NDOCS, dtype=jnp.int32)
    before_big = smaller[jnp.clip(places, 0, NDOCS - 2)]
    after_big = smaller[jnp.clip(places - 1, 0, NDOCS - 2)]
    return jnp.where(places < big_spot, before_big, jnp.where(places == big_spot, DOC_MOST, after_big)).astype(jnp.int32)


def draw_doc_lengths(key, part):
    lengths_drawn = doc_plan(key)
    return lengths_drawn


def draw_owner_lists(key, part):
    lengths_drawn = doc_plan(key)
    key = jax.random.fold_in(key, 5)
    doc_ends = jnp.cumsum(lengths_drawn)
    doc_begins = doc_ends - lengths_drawn
    positions = jnp.arange(SEQ, dtype=jnp.int32)
    firsts = jnp.max(jnp.where(doc_begins[None, :] <= positions[:, None], doc_begins[None, :], 0), axis=1)
    stretch_cost = jnp.sum((positions - firsts + 1).reshape(2 * N_CTX, STRETCH), axis=1).astype(jnp.int32)
    ranking = jnp.argsort(stretch_cost * (2 * N_CTX) + jnp.arange(2 * N_CTX, dtype=jnp.int32)).astype(jnp.int32)
    paired = jnp.stack([ranking[:N_CTX], ranking[::-1][:N_CTX]], axis=1)
    flipped = jax.random.randint(jax.random.fold_in(key, 1), (N_CTX,), 0, 2)
    paired = jnp.where(flipped[:, None] == 1, paired[:, ::-1], paired)
    owner_order = jax.random.permutation(jax.random.fold_in(key, 2), N_CTX)
    return paired[jnp.argsort(owner_order)].astype(jnp.int32)


def draw_queries(key, part):
    key = jax.random.fold_in(key, 1)
    base = jnp.clip(jax.random.normal(key, (SEQ, Q_HEADS * HEAD_DIM), jnp.float32), -6.0, 6.0)
    return base.astype(jnp.bfloat16)


def draw_keys(key, part):
    key = jax.random.fold_in(key, 2)
    base = jnp.clip(jax.random.normal(key, (SEQ, KV_HEADS * HEAD_DIM), jnp.float32), -6.0, 6.0)
    return base.astype(jnp.bfloat16)


def shard_levels(rng, dims, split, low, high):
    loudness, own = 1.0, jax.random.fold_in(rng, 6)
    for position, blocks in split:
        steps = jnp.exp(jax.random.uniform(jax.random.fold_in(own, position), (blocks,), jnp.float32, low / len(split), high / len(split)))
        loudness = loudness * jnp.repeat(steps, dims[position] // blocks).reshape([-1 if axis == position else 1 for axis in range(len(dims))])
    return loudness


def bell_draw(rng, dims, scale, limit, cuts=(), held_as=jnp.bfloat16):
    factor_of = shard_levels(rng, dims, cuts, -0.22, 0.18) if cuts else 1.0
    array = jax.random.normal(rng, dims, jnp.float32) * scale * factor_of
    return jnp.minimum(jnp.maximum(array, -limit), limit).astype(held_as)


def setup_inputs(seed: int = 0) -> dict:
    seeds = jax.random.split(jax.random.key(seed), 7)
    return {
        "queries": draw_queries(jax.random.fold_in(seeds[6], 71), 0),
        "keys": draw_keys(jax.random.fold_in(seeds[6], 71), 0),
        "values": bell_draw(seeds[2], (SEQ, KV_HEADS * HEAD_DIM), 1.0, 6.0, ((0, 128),)),
        "grad_out": bell_draw(seeds[3], (SEQ, Q_HEADS * HEAD_DIM), 1.0, 6.0, ((0, 32), (1, 4))),
        "owner_lists": draw_owner_lists(jax.random.fold_in(seeds[6], 71), 0),
        "doc_lengths": draw_doc_lengths(jax.random.fold_in(seeds[6], 71), 0),
    }


def reference(queries, keys, values, grad_out, owner_lists, doc_lengths):
    score_scale = 1.0 / math.sqrt(HEAD_DIM)
    col_width = GROUP * HEAD_DIM
    owner_pos = (owner_lists[:, :, None] * STRETCH + jnp.arange(STRETCH, dtype=jnp.int32)[None, None, :]).reshape(N_CTX, TOK_DEV)
    owner_pos = owner_pos.astype(jnp.int32)
    doc_ends = jnp.cumsum(doc_lengths)
    doc_begins = doc_ends - doc_lengths
    positions = jnp.arange(SEQ, dtype=jnp.int32)
    doc_first = lax.optimization_barrier(jnp.max(jnp.where(doc_begins[None, :] <= positions[:, None], doc_begins[None, :], 0), axis=1))

    def per_owner(carry, inputs):
        own_pos, own_grads = inputs
        own_queries = queries[own_pos]
        row_pos = jnp.repeat(own_pos, GROUP)
        row_first = doc_first[row_pos]
        visible = (positions[None, :] <= row_pos[:, None]) & (positions[None, :] >= row_first[:, None])
        key_sum, value_sum = carry
        outputs, query_grads, key_parts, value_parts = ([], [], [], [])
        for kv_head in range(KV_HEADS):
            head_cols = slice(kv_head * col_width, (kv_head + 1) * col_width)
            kv_cols = slice(kv_head * HEAD_DIM, (kv_head + 1) * HEAD_DIM)
            query_rows = own_queries[:, head_cols].reshape(TOK_DEV * GROUP, HEAD_DIM)
            grad_rows = own_grads[:, head_cols].reshape(TOK_DEV * GROUP, HEAD_DIM)
            key_rows = keys[:, kv_cols]
            value_rows = values[:, kv_cols]
            scores = jnp.dot(query_rows, key_rows.T, preferred_element_type=jnp.float32) * score_scale
            peak_score = lax.optimization_barrier(jnp.max(jnp.where(visible, scores, -jnp.inf), axis=1, keepdims=True))
            exp_total = lax.optimization_barrier(jnp.sum(jnp.exp(jnp.where(visible, scores - peak_score, -jnp.inf)), axis=1, keepdims=True))
            log_sum = peak_score + jnp.log(exp_total)
            weights = jnp.exp(jnp.where(visible, scores - log_sum, -jnp.inf))
            rounded = weights.astype(jnp.bfloat16)
            attention = jnp.dot(rounded, value_rows, preferred_element_type=jnp.float32).astype(jnp.bfloat16)
            delta = lax.optimization_barrier(jnp.sum(grad_rows.astype(jnp.float32) * attention.astype(jnp.float32), axis=1, keepdims=True))
            pushed = jnp.dot(grad_rows, value_rows.T, preferred_element_type=jnp.float32)
            slopes = (weights * (pushed - delta)).astype(jnp.bfloat16)
            query_grad = (jnp.dot(slopes, key_rows, preferred_element_type=jnp.float32) * score_scale).astype(jnp.bfloat16)
            key_parts.append((jnp.dot(slopes.T, query_rows, preferred_element_type=jnp.float32) * score_scale).astype(jnp.bfloat16))
            value_parts.append(jnp.dot(rounded.T, grad_rows, preferred_element_type=jnp.float32).astype(jnp.bfloat16))
            outputs.append(attention.reshape(TOK_DEV, col_width))
            query_grads.append(query_grad.reshape(TOK_DEV, col_width))
        key_sum = key_sum + jnp.concatenate(key_parts, axis=1).astype(jnp.float32)
        value_sum = value_sum + jnp.concatenate(value_parts, axis=1).astype(jnp.float32)
        return ((key_sum, value_sum), (jnp.concatenate(outputs, axis=1), jnp.concatenate(query_grads, axis=1)))
    zeros_kv = jnp.zeros((SEQ, KV_HEADS * HEAD_DIM), jnp.float32)
    grads_owner = grad_out.reshape(N_CTX, TOK_DEV, Q_HEADS * HEAD_DIM)
    sums, stacked = lax.scan(per_owner, (zeros_kv, zeros_kv), (owner_pos, grads_owner))
    attn_out = stacked[0].reshape(SEQ, Q_HEADS * HEAD_DIM)
    grad_q = jnp.zeros((SEQ, Q_HEADS * HEAD_DIM), jnp.bfloat16).at[owner_pos.reshape(SEQ)].set(stacked[1].reshape(SEQ, Q_HEADS * HEAD_DIM))
    return (attn_out, grad_q, sums[0].astype(jnp.bfloat16), sums[1].astype(jnp.bfloat16))
```

```python
import functools
import math

import jax
import jax.numpy as jnp
from jax import lax
from jax.experimental import pallas as pl
from jax.experimental.pallas import tpu as pltpu
from jax.sharding import PartitionSpec as P

MESH = pl.DeviceIdType.MESH
BF16 = jnp.bfloat16
F32 = jnp.float32

N_CTX, N_HEAD = 32, 4
NZ, NY, NCORE = 4, 4, 2
PLANE = NY * NCORE
PLANES = 3
WINDOW = 17
TOK = 128
PART = 32
DIM = 128
GROUP = 8
ROWS = TOK * GROUP
COLS = GROUP * DIM
NDOCS = 16
MASKED = -1e30
SCALE = 1.0 / math.sqrt(DIM)
LOG2E = 1.0 / math.log(2.0)

XK, XV, XQ, G1, G2, A1, A2, DQ, DK, DV = range(10)
Z1, Z2, Y0, C0, CP, YP, ZP = 10, 11, 12, 15, 18, 21, 24
N_SEM = 26
LQ, LK, LV, LG, LA, LDQ, LDK, LDV = range(8)
N_LOCAL = 8


def body(
    q_in, k_in, v_in, go_in, slot_of, owned, doc_lengths,
    ao, gq, gk, gv,
    kv, qs, gcol, gperm, gos, acol, aperm, out_rows, dq_rows,
    q_rows, q_cols, go_cols, probs, parts, from_core, y_sum, from_y, z_sum, from_z, grads,
    send, recv, local,
):
    c = lax.axis_index("ctx")
    h = lax.axis_index("head")
    z = c // PLANE
    idx = lax.rem(c, PLANE)
    y = idx // NCORE
    co = lax.rem(idx, NCORE)
    sib = c + 1 - 2 * co
    tile_row = pl.multiple_of(16 * (c // GROUP), 16)
    tile_head = lax.rem(c, GROUP)

    def ctx_at(zz, yy):
        return lax.rem(zz, NZ) * PLANE + lax.rem(yy, NY) * NCORE + co

    def push(src, dst, sem, ctx, head):
        copy = pltpu.make_async_remote_copy(
            src_ref=src, dst_ref=dst, send_sem=send.at[sem], recv_sem=recv.at[sem],
            device_id=(ctx, head), device_id_type=MESH,
        )
        copy.start()

    def drain(ref, sem):
        pltpu.make_async_copy(ref, ref, sem).wait()

    def cols(number, width):
        return pl.ds(pl.multiple_of(number * width, width), width)

    local_copies = [
        pltpu.make_async_copy(k_in.at[:, cols(h, DIM)], kv.at[2, y, co, 0, cols(h, PART), :], local.at[LK]),
        pltpu.make_async_copy(v_in.at[:, cols(h, DIM)], kv.at[2, y, co, 1, cols(h, PART), :], local.at[LV]),
        pltpu.make_async_copy(q_in.at[:, cols(h, COLS)], qs.at[cols(h, PART), :], local.at[LQ]),
        pltpu.make_async_copy(
            go_in.at[:, pl.ds(tile_row, 16), cols(tile_head, DIM)], gcol.at[pl.ds(2 * c, 2)], local.at[LG]
        ),
    ]
    for copy in local_copies:
        copy.start()

    barrier = pltpu.get_barrier_semaphore()

    def greet(step, carry):
        pl.semaphore_signal(barrier, inc=1, device_id=(lax.rem(c + step, N_CTX), h), device_id_type=MESH)
        return carry

    lax.fori_loop(1, N_CTX, greet, 0)
    for step in range(1, N_HEAD):
        pl.semaphore_signal(barrier, inc=1, device_id=(c, lax.rem(h + step, N_HEAD)), device_id_type=MESH)
    pl.semaphore_wait(barrier, N_CTX - 1 + N_HEAD - 1)

    for step in range(1, N_HEAD):
        to = lax.rem(h + step, N_HEAD)
        push(k_in.at[:, cols(to, DIM)], kv.at[2, y, co, 0, cols(h, PART), :], XK, c, to)
        push(v_in.at[:, cols(to, DIM)], kv.at[2, y, co, 1, cols(h, PART), :], XV, c, to)
    for step in range(1, N_HEAD):
        to = lax.rem(h + step, N_HEAD)
        push(q_in.at[:, cols(to, COLS)], qs.at[cols(h, PART), :], XQ, c, to)

    def tile_of(number):
        return pl.multiple_of(16 * (number // GROUP), 16), lax.rem(number, GROUP)

    def collect_grad(step, carry):
        to = lax.rem(c + step, N_CTX)
        row, head = tile_of(to)
        push(go_in.at[:, pl.ds(row, 16), cols(head, DIM)], gcol.at[pl.ds(2 * c, 2)], G1, to, h)
        return carry

    lax.fori_loop(1, N_CTX, collect_grad, 0)

    own = kv.at[2, y, co]
    local_copies[0].wait()
    local_copies[1].wait()
    drain(kv.at[2, y, co, 0, pl.ds(0, 3 * PART), :], recv.at[XK])
    drain(kv.at[2, y, co, 1, pl.ds(0, 3 * PART), :], recv.at[XV])
    push(own, kv.at[1, y, co], Z1, ctx_at(z + 1, y), h)
    push(own, kv.at[0, y, co], Z2, ctx_at(z + 2, y), h)

    def along_y(plane):
        for step in range(1, NY):
            push(kv.at[plane, y, co], kv.at[plane, y, co], Y0 + plane, ctx_at(z, y + step), h)

    along_y(2)

    local_copies[3].wait()
    drain(gcol.at[pl.ds(0, 62)], recv.at[G1])

    def arrange_grad(number, carry):
        gperm[number] = gcol[slot_of[number]]
        return carry

    lax.fori_loop(0, 2 * N_CTX, arrange_grad, 0)

    def deliver_grad(step, carry):
        to = lax.rem(c + step, N_CTX)
        push(
            gperm.at[pl.ds(2 * to, 2)], gos.at[tile_head, :, pl.ds(tile_row, 16), :], G2, to, h
        )
        return carry

    lax.fori_loop(1, N_CTX, deliver_grad, 0)
    gos[tile_head, :, pl.ds(tile_row, 16), :] = gperm[pl.ds(2 * c, 2)]

    drain(kv.at[1, y, co], recv.at[Z1])
    along_y(1)
    drain(kv.at[0, y, co], recv.at[Z2])
    along_y(0)
    for plane in (2, 1, 0):
        drain(kv.at[plane, pl.ds(0, 3), co], recv.at[Y0 + plane])
        push(kv.at[plane, :, co], kv.at[plane, :, co], C0 + plane, sib, h)

    local_copies[2].wait()
    drain(qs.at[pl.ds(0, 3 * PART), :], recv.at[XQ])
    for head in range(GROUP):
        rows = qs[:, head * DIM : (head + 1) * DIM]
        q_rows[head * TOK : (head + 1) * TOK, :] = rows
        q_cols[:, head * TOK : (head + 1) * TOK] = rows.T

    q_pos = c * TOK + lax.broadcasted_iota(jnp.int32, (1, TOK), 1)
    first = jnp.zeros((1, TOK), jnp.int32)
    begin = jnp.int32(0)
    for doc in range(NDOCS):
        first = jnp.where(q_pos >= begin, jnp.maximum(first, begin), first)
        begin = begin + doc_lengths[doc]

    parts[0] = jnp.zeros(parts.shape[1:], BF16)
    parts[2] = jnp.zeros(parts.shape[1:], BF16)

    for plane in (2, 1, 0):
        drain(kv.at[plane, :, co], recv.at[C0 + plane])

    def split(flat):
        return flat // PLANE, lax.rem(flat // NCORE, NY), lax.rem(flat, NCORE)

    def scores(step, peak):
        plane, yy, core = split(idx + step)
        keys = kv[plane, yy, core, 0]
        key_pos = (c - (WINDOW - 1) + step) * TOK + lax.broadcasted_iota(jnp.int32, (TOK, TOK), 0)
        bias = jnp.where((key_pos <= q_pos) & (key_pos >= first), 0.0, MASKED)
        bias = jnp.concatenate([bias] * GROUP, axis=1)
        block = jnp.dot(keys, q_cols[...], preferred_element_type=F32) * (SCALE * LOG2E) + bias
        probs[step] = block
        return jnp.maximum(peak, jnp.max(block, axis=0, keepdims=True))

    peak = lax.fori_loop(0, WINDOW, scores, jnp.full((1, ROWS), MASKED, F32))

    def attend(step, carry):
        total, accum = carry
        plane, yy, core = split(idx + step)
        values = kv[plane, yy, core, 1]
        block = jnp.exp2(probs[step] - peak)
        probs[step] = block
        total = total + jnp.sum(block, axis=0, keepdims=True)
        accum = accum + jnp.dot(values.T, block.astype(BF16), preferred_element_type=F32)
        return total, accum

    total, accum = lax.fori_loop(
        0, WINDOW, attend, (jnp.zeros((1, ROWS), F32), jnp.zeros((DIM, ROWS), F32))
    )
    inverse = 1.0 / total
    rounded = (accum * inverse).astype(BF16)
    for head in range(GROUP):
        rows = rounded[:, head * TOK : (head + 1) * TOK].T
        out_rows[head, 0] = rows[:64]
        out_rows[head, 1] = rows[64:]

    def collect_out(step, carry):
        to = lax.rem(c + step, N_CTX)
        row, head = tile_of(to)
        push(out_rows.at[head, :, pl.ds(row, 16), :], acol.at[pl.ds(2 * c, 2)], A1, to, h)
        return carry

    lax.fori_loop(1, N_CTX, collect_out, 0)
    acol[pl.ds(2 * c, 2)] = out_rows[tile_head, :, pl.ds(tile_row, 16), :]

    drain(gperm.at[pl.ds(0, 62)], recv.at[G2])
    for head in range(GROUP):
        go_cols[:, head * TOK : (head + 1) * TOK] = gos[head].reshape(TOK, DIM).T
    delta = jnp.sum(go_cols[...].astype(F32) * rounded.astype(F32), axis=0, keepdims=True)

    def backward(flat, query_grad):
        plane, yy, core = split(flat)
        keys, values = kv[plane, yy, core, 0], kv[plane, yy, core, 1]
        weights = probs[flat - idx] * inverse
        pushed = jnp.dot(values, go_cols[...], preferred_element_type=F32)
        slopes = (weights * (pushed - delta)).astype(BF16)
        go_rows = gos[...].reshape(ROWS, DIM)
        key_part = jnp.dot(slopes, q_rows[...], preferred_element_type=F32) * SCALE
        value_part = jnp.dot(weights.astype(BF16), go_rows, preferred_element_type=F32)
        parts[plane, yy, core, 0] = key_part.astype(BF16)
        parts[plane, yy, core, 1] = value_part.astype(BF16)
        return query_grad + jnp.dot(keys.T, slopes, preferred_element_type=F32)

    def to_core(plane):
        push(parts.at[plane, :, 1 - co], from_core.at[plane], CP + plane, sib, h)

    def to_y(plane):
        drain(from_core.at[plane], recv.at[CP + plane])
        mine = parts[plane, :, co].astype(F32) + from_core[plane].astype(F32)
        y_sum[plane] = mine.astype(BF16)
        for step in range(1, NY):
            other = lax.rem(y + step, NY)
            push(y_sum.at[plane, other], from_y.at[plane, step - 1], YP + plane, ctx_at(z, y + step), h)

    def sum_y(plane):
        drain(from_y.at[plane], recv.at[YP + plane])
        total = y_sum[plane, y].astype(F32)
        for step in range(NY - 1):
            total = total + from_y[plane, step].astype(F32)
        return total

    def to_z(plane):
        z_sum[plane] = sum_y(plane).astype(BF16)
        push(z_sum.at[plane], from_z.at[plane], ZP + plane, ctx_at(z + 2 + plane, y), h)

    query_grad = jnp.zeros((DIM, ROWS), F32)
    query_grad = lax.fori_loop(idx, PLANE, backward, query_grad)
    to_core(0)

    drain(acol.at[pl.ds(0, 62)], recv.at[A1])

    def arrange_out(number, carry):
        aperm[number] = acol[owned[number]]
        return carry

    lax.fori_loop(0, 2 * N_CTX, arrange_out, 0)

    def deliver_out(step, carry):
        to = lax.rem(c + step, N_CTX)
        push(
            aperm.at[pl.ds(2 * to, 2)], ao.at[:, pl.ds(tile_row, 16), cols(tile_head, DIM)], A2, to, h
        )
        return carry

    lax.fori_loop(1, N_CTX, deliver_out, 0)
    own_out = pltpu.make_async_copy(
        aperm.at[pl.ds(2 * c, 2)], ao.at[:, pl.ds(tile_row, 16), cols(tile_head, DIM)], local.at[LA]
    )
    own_out.start()

    query_grad = lax.fori_loop(PLANE, 2 * PLANE, backward, query_grad)
    to_core(1)
    to_y(0)
    query_grad = lax.fori_loop(2 * PLANE, 2 * PLANE + idx + 1, backward, query_grad)
    to_core(2)
    to_y(1)

    query_grad = (query_grad * SCALE).astype(BF16)
    for head in range(GROUP):
        dq_rows[:, head * DIM : (head + 1) * DIM] = query_grad[:, head * TOK : (head + 1) * TOK].T
    for step in range(1, N_HEAD):
        to = lax.rem(h + step, N_HEAD)
        push(dq_rows.at[cols(to, PART), :], gq.at[:, cols(h, COLS)], DQ, c, to)
    own_dq = pltpu.make_async_copy(dq_rows.at[cols(h, PART), :], gq.at[:, cols(h, COLS)], local.at[LDQ])
    own_dq.start()

    to_y(2)
    to_z(0)
    to_z(1)
    home = sum_y(2)
    for plane in (1, 0):
        drain(from_z.at[plane], recv.at[ZP + plane])
        home = home + from_z[plane].astype(F32)
    grads[...] = home.astype(BF16)
    for step in range(1, N_HEAD):
        to = lax.rem(h + step, N_HEAD)
        push(grads.at[0, cols(to, PART), :], gk.at[:, cols(h, DIM)], DK, c, to)
        push(grads.at[1, cols(to, PART), :], gv.at[:, cols(h, DIM)], DV, c, to)
    own_dk = pltpu.make_async_copy(grads.at[0, cols(h, PART), :], gk.at[:, cols(h, DIM)], local.at[LDK])
    own_dv = pltpu.make_async_copy(grads.at[1, cols(h, PART), :], gv.at[:, cols(h, DIM)], local.at[LDV])
    own_dk.start()
    own_dv.start()

    three_cols = pl.ds(0, 3 * COLS)
    drain(gperm.at[pl.ds(0, 62)], recv.at[A2])
    drain(gq.at[:, three_cols], recv.at[DQ])
    drain(gk.at[:, pl.ds(0, 3 * DIM)], recv.at[DK])
    drain(gv.at[:, pl.ds(0, 3 * DIM)], recv.at[DV])
    for copy in (own_out, own_dq, own_dk, own_dv):
        copy.wait()
    drain(kv.at[0, 0, 0, 0, pl.ds(0, 3 * PART), :], send.at[XK])
    drain(kv.at[0, 0, 0, 0, pl.ds(0, 3 * PART), :], send.at[XV])
    for sem in (G1, G2, A1, A2):
        drain(gperm.at[pl.ds(0, 62)], send.at[sem])
    for sem in (XQ, DQ):
        drain(gq.at[:, three_cols], send.at[sem])
    for sem in (DK, DV):
        drain(gk.at[:, pl.ds(0, 3 * DIM)], send.at[sem])
    for sem in (Z1, Z2, ZP, ZP + 1):
        drain(z_sum.at[0], send.at[sem])
    for plane in range(PLANES):
        drain(from_y.at[0], send.at[Y0 + plane])
        drain(from_y.at[0], send.at[YP + plane])
        drain(from_core.at[0], send.at[C0 + plane])
        drain(from_core.at[0], send.at[CP + plane])


def shards(queries, keys, values, grad_out, owner_lists, doc_lengths):
    owned = owner_lists.reshape(2 * N_CTX)
    slots = lax.iota(jnp.int32, 2 * N_CTX)
    slot_of = jnp.sum(jnp.where(owned[None, :] == slots[:, None], slots[None, :], 0), axis=1)
    hbm = pl.BlockSpec(memory_space=pl.ANY)
    smem = pl.BlockSpec(memory_space=pltpu.SMEM)
    block = (2, TOK, DIM)
    ao, gq, gk, gv = pl.pallas_call(
        body,
        out_shape=(
            jax.ShapeDtypeStruct((2, TOK // 2, COLS), BF16),
            jax.ShapeDtypeStruct((PART, N_HEAD * COLS), BF16),
            jax.ShapeDtypeStruct((PART, N_HEAD * DIM), BF16),
            jax.ShapeDtypeStruct((PART, N_HEAD * DIM), BF16),
        ),
        in_specs=[hbm] * 4 + [smem] * 3,
        out_specs=(hbm,) * 4,
        scratch_shapes=[
            pltpu.VMEM((PLANES, NY, NCORE) + block, BF16),
            pltpu.VMEM((TOK, COLS), BF16),
            pltpu.VMEM((2 * N_CTX, 16, DIM), BF16),
            pltpu.VMEM((2 * N_CTX, 16, DIM), BF16),
            pltpu.VMEM((GROUP, 2, TOK // 2, DIM), BF16),
            pltpu.VMEM((2 * N_CTX, 16, DIM), BF16),
            pltpu.VMEM((2 * N_CTX, 16, DIM), BF16),
            pltpu.VMEM((GROUP, 2, TOK // 2, DIM), BF16),
            pltpu.VMEM((TOK, COLS), BF16),
            pltpu.VMEM((ROWS, DIM), BF16),
            pltpu.VMEM((DIM, ROWS), BF16),
            pltpu.VMEM((DIM, ROWS), BF16),
            pltpu.VMEM((WINDOW, TOK, ROWS), F32),
            pltpu.VMEM((PLANES, NY, NCORE) + block, BF16),
            pltpu.VMEM((PLANES, NY) + block, BF16),
            pltpu.VMEM((PLANES, NY) + block, BF16),
            pltpu.VMEM((PLANES, NY - 1) + block, BF16),
            pltpu.VMEM((2,) + block, BF16),
            pltpu.VMEM((2,) + block, BF16),
            pltpu.VMEM(block, BF16),
            pltpu.SemaphoreType.DMA((N_SEM,)),
            pltpu.SemaphoreType.DMA((N_SEM,)),
            pltpu.SemaphoreType.DMA((N_LOCAL,)),
        ],
        compiler_params=pltpu.CompilerParams(
            collective_id=0, has_side_effects=True, vmem_limit_bytes=48 * 1024 * 1024
        ),
        cost_estimate=pl.CostEstimate(flops=4_000_000_000, bytes_accessed=4_000_000, transcendentals=2_300_000),
        name="attention_core",
    )(queries, keys, values, grad_out.reshape(2, TOK // 2, COLS), slot_of, owned, doc_lengths)
    return ao.reshape(TOK, COLS), gq, gk, gv


def solution(mesh):
    placed = (
        P(("ctx", "head"), None),
        P(("ctx", "head"), None),
        P(("ctx", "head"), None),
        P("ctx", "head"),
        P(),
        P(),
    )
    return jax.shard_map(
        shards,
        mesh=mesh,
        in_specs=placed,
        out_specs=(
            P("ctx", "head"),
            P(("ctx", "head"), None),
            P(("ctx", "head"), None),
            P(("ctx", "head"), None),
        ),
        check_vma=False,
    )
```

```python
import functools
import math

import jax
import jax.numpy as jnp
from jax import lax
from jax.experimental import pallas as pl
from jax.experimental.pallas import tpu as pltpu
from jax.sharding import PartitionSpec as P

MESH = pl.DeviceIdType.MESH
BF16 = jnp.bfloat16
F32 = jnp.float32

N_CTX, N_HEAD = 32, 4
NZ, NY, NCORE = 4, 4, 2
PLANE = NY * NCORE
PLANES = 3
SLOTS = 9
PAIR = 256
TOK = 128
PART = 32
DIM = 128
GROUP = 8
ROWS = TOK * GROUP
COLS = GROUP * DIM
NDOCS = 16
MASKED = -1e30
SCALE = 1.0 / math.sqrt(DIM)
LOG2E = 1.0 / math.log(2.0)

X0, X1, X2, Y1, YV, C1, CV, XQ, G1, G2, A1, A2, DQ, CP, YP1, YPV, XP = *range(14), 16, 17, 18
N_SEM = 21
LK, LV, LRK, LRV, LQ, LG, LA, LDQ, LDK, LDV = range(10)
N_LOCAL = 10


def body(
    q_in, k_in, v_in, go_in, owned, doc_lengths,
    ao, gq, gk, gv,
    raw, kv, qs, gcol, gperm, gos, acol, aperm, out_rows, dq_rows,
    q_rows, q_cols, go_cols, probs, parts, from_core, y_sum, from_y, x_sum, from_x, grads,
    slot_vec, slot_of, send, recv, local,
):
    c = lax.axis_index("ctx")
    h = lax.axis_index("head")
    z = c // PLANE
    idx = lax.rem(c, PLANE)
    y = idx // NCORE
    co = lax.rem(idx, NCORE)
    sib = c + 1 - 2 * co
    tile_row = pl.multiple_of(16 * (c // GROUP), 16)
    tile_head = lax.rem(c, GROUP)

    def ctx_at(zz, yy):
        return lax.rem(zz, NZ) * PLANE + lax.rem(yy, NY) * NCORE + co

    def push(src, dst, sem, ctx, head):
        copy = pltpu.make_async_remote_copy(
            src_ref=src, dst_ref=dst, send_sem=send.at[sem], recv_sem=recv.at[sem],
            device_id=(ctx, head), device_id_type=MESH,
        )
        copy.start()

    def drain(ref, sem):
        pltpu.make_async_copy(ref, ref, sem).wait()

    def cols(number, width):
        return pl.ds(pl.multiple_of(number * width, width), width)

    own_slot = NY + y

    local_copies = [
        pltpu.make_async_copy(k_in.at[:, cols(h, DIM)], kv.at[own_slot, co, 0, cols(h, PART), :], local.at[LK]),
        pltpu.make_async_copy(v_in.at[:, cols(h, DIM)], kv.at[own_slot, co, 1, cols(h, PART), :], local.at[LV]),
        pltpu.make_async_copy(k_in, raw.at[0], local.at[LRK]),
        pltpu.make_async_copy(v_in, raw.at[1], local.at[LRV]),
        pltpu.make_async_copy(q_in.at[:, cols(h, COLS)], qs.at[cols(h, PART), :], local.at[LQ]),
        pltpu.make_async_copy(
            go_in.at[:, pl.ds(tile_row, 16), cols(tile_head, DIM)], gcol.at[pl.ds(2 * c, 2)], local.at[LG]
        ),
    ]
    for copy in local_copies:
        copy.start()

    barrier = pltpu.get_barrier_semaphore()

    def greet(step, carry):
        pl.semaphore_signal(barrier, inc=1, device_id=(lax.rem(c + step, N_CTX), h), device_id_type=MESH)
        return carry

    lax.fori_loop(1, N_CTX, greet, 0)
    for step in range(1, N_HEAD):
        pl.semaphore_signal(barrier, inc=1, device_id=(c, lax.rem(h + step, N_HEAD)), device_id_type=MESH)
        for ahead in (1, 2, 3):
            pl.semaphore_signal(
                barrier, inc=1, device_id=(ctx_at(z + ahead, y), lax.rem(h + step, N_HEAD)), device_id_type=MESH
            )

    lanes = lax.broadcasted_iota(jnp.int32, (8, DIM), 1)
    found = jnp.zeros((8, DIM), jnp.int32)
    for number in range(2 * N_CTX):
        found = jnp.where(lanes == owned[number // 2, number % 2], number, found)
    slot_vec[...] = found
    slot_copy = pltpu.make_async_copy(slot_vec, slot_of, local.at[LA])
    slot_copy.start()

    for copy in local_copies[:4]:
        copy.wait()
    slot_copy.wait()
    pl.semaphore_wait(barrier, N_CTX - 1 + 4 * (N_HEAD - 1))

    def by_head(slot, sem, ctx, first_step):
        for step in range(first_step, N_HEAD):
            to = lax.rem(h + step, N_HEAD)
            push(raw.at[:, :, cols(to, DIM)], kv.at[slot, co, :, cols(h, PART), :], sem, ctx, to)

    by_head(own_slot, X0, c, 1)
    by_head(y, X1, ctx_at(z + 1, y), 0)
    by_head(2 * NY, X2, ctx_at(z + 2, y), 0)
    for step in range(1, N_HEAD):
        to = lax.rem(h + step, N_HEAD)
        push(q_in.at[:, cols(to, COLS)], qs.at[cols(h, PART), :], XQ, c, to)

    drain(kv.at[0, 0, :, pl.ds(0, 3 * PART), :], recv.at[X0])
    for step in range(1, NY):
        yy = lax.rem(y + step, NY)

        @pl.when(yy > y)
        def _():
            push(kv.at[own_slot, co], kv.at[own_slot, co], YV, ctx_at(z, yy), h)

    drain(kv.at[0, 0], recv.at[X1])
    for step in range(1, NY):
        push(kv.at[y, co], kv.at[y, co], Y1, ctx_at(z, y + step), h)
    drain(kv.at[0, 0], recv.at[X2])
    for step in range(1, NY):
        yy = lax.rem(y + step, NY)

        @pl.when(yy < y)
        def _():
            push(kv.at[2 * NY, co], kv.at[own_slot, co], YV, ctx_at(z, yy), h)

    def tile_of(number):
        return pl.multiple_of(16 * (number // GROUP), 16), lax.rem(number, GROUP)

    def collect_grad(step, carry):
        to = lax.rem(c + step, N_CTX)
        row, head = tile_of(to)
        push(go_in.at[:, pl.ds(row, 16), cols(head, DIM)], gcol.at[pl.ds(2 * c, 2)], G1, to, h)
        return carry

    lax.fori_loop(1, N_CTX, collect_grad, 0)

    local_copies[4].wait()
    drain(qs.at[pl.ds(0, 3 * PART), :], recv.at[XQ])
    for head in range(GROUP):
        rows = qs[:, head * DIM : (head + 1) * DIM]
        q_rows[head * TOK : (head + 1) * TOK, :] = rows
        q_cols[:, head * TOK : (head + 1) * TOK] = rows.T

    q_pos = c * TOK + lax.broadcasted_iota(jnp.int32, (1, TOK), 1)
    first = jnp.zeros((1, TOK), jnp.int32)
    begin = jnp.int32(0)
    for doc in range(NDOCS):
        first = jnp.where(q_pos >= begin, jnp.maximum(first, begin), first)
        begin = begin + doc_lengths[doc]

    drain(kv.at[pl.ds(0, 3), 0], recv.at[Y1])
    push(kv.at[pl.ds(0, NY), co], kv.at[pl.ds(0, NY), co], C1, sib, h)
    drain(kv.at[pl.ds(0, 3), 0], recv.at[YV])
    push(kv.at[pl.ds(NY, NY + 1), co], kv.at[pl.ds(NY, NY + 1), co], CV, sib, h)

    local_copies[5].wait()
    drain(gcol.at[pl.ds(0, 62)], recv.at[G1])

    def arrange_grad(number, carry):
        gperm[number] = gcol[slot_of[0, number]]
        return carry

    lax.fori_loop(0, 2 * N_CTX, arrange_grad, 0, unroll=8)

    def deliver_grad(step, carry):
        to = lax.rem(c + step, N_CTX)
        push(
            gperm.at[pl.ds(2 * to, 2)], gos.at[tile_head, :, pl.ds(tile_row, 16), :], G2, to, h
        )
        return carry

    lax.fori_loop(1, N_CTX, deliver_grad, 0)
    gos[tile_head, :, pl.ds(tile_row, 16), :] = gperm[pl.ds(2 * c, 2)]

    def position(slot):
        if slot < NY:
            return ((z - 1) * NY + slot) * PAIR
        if slot < 2 * NY:
            return (jnp.where(slot - NY <= y, z, z - 2) * NY + slot - NY) * PAIR
        return ((z - 2) * NY + y) * PAIR

    def scores(slot, peak):
        keys = kv[slot, :, 0].reshape(PAIR, DIM)
        key_pos = position(slot) + lax.broadcasted_iota(jnp.int32, (PAIR, TOK), 0)
        bias = jnp.where((key_pos <= q_pos) & (key_pos >= first), 0.0, MASKED)
        bias = jnp.concatenate([bias] * GROUP, axis=1)
        block = jnp.dot(keys, q_cols[...], preferred_element_type=F32) * (SCALE * LOG2E) + bias
        probs[slot] = block
        return jnp.maximum(peak, jnp.max(block.reshape(PAIR // 8, 8, ROWS), axis=0))

    peak = jnp.full((8, ROWS), MASKED, F32)
    drain(kv.at[pl.ds(0, NY), 0], recv.at[C1])
    for slot in range(NY):
        peak = scores(slot, peak)
    drain(kv.at[pl.ds(0, NY + 1), 0], recv.at[CV])
    for slot in range(NY, SLOTS):
        peak = scores(slot, peak)
    peak = jnp.max(peak, axis=0, keepdims=True)

    total = jnp.zeros((8, ROWS), F32)
    accum = jnp.zeros((DIM, ROWS), F32)
    for slot in range(SLOTS):
        values = kv[slot, :, 1].reshape(PAIR, DIM)
        block = jnp.exp2(probs[slot] - peak)
        probs[slot] = block
        total = total + jnp.sum(block.reshape(PAIR // 8, 8, ROWS), axis=0)
        accum = accum + jnp.dot(values.T, block.astype(BF16), preferred_element_type=F32)
    inverse = 1.0 / jnp.sum(total, axis=0, keepdims=True)
    rounded = (accum * inverse).astype(BF16)
    for head in range(GROUP):
        rows = rounded[:, head * TOK : (head + 1) * TOK].T
        out_rows[head, 0] = rows[:64]
        out_rows[head, 1] = rows[64:]

    def collect_out(step, carry):
        to = lax.rem(c + step, N_CTX)
        row, head = tile_of(to)
        push(out_rows.at[head, :, pl.ds(row, 16), :], acol.at[pl.ds(2 * c, 2)], A1, to, h)
        return carry

    lax.fori_loop(1, N_CTX, collect_out, 0)
    acol[pl.ds(2 * c, 2)] = out_rows[tile_head, :, pl.ds(tile_row, 16), :]

    drain(gperm.at[pl.ds(0, 62)], recv.at[G2])
    for head in range(GROUP):
        go_cols[:, head * TOK : (head + 1) * TOK] = gos[head].reshape(TOK, DIM).T
    delta = jnp.sum(go_cols[...].astype(F32) * rounded.astype(F32), axis=0, keepdims=True)

    def backward(slot, query_grad):
        keys, values = kv[slot, :, 0].reshape(PAIR, DIM), kv[slot, :, 1].reshape(PAIR, DIM)
        weights = probs[slot] * inverse
        pushed = jnp.dot(values, go_cols[...], preferred_element_type=F32)
        slopes = (weights * (pushed - delta)).astype(BF16)
        go_rows = gos[...].reshape(ROWS, DIM)
        key_part = jnp.dot(slopes, q_rows[...], preferred_element_type=F32) * SCALE
        value_part = jnp.dot(weights.astype(BF16), go_rows, preferred_element_type=F32)
        parts[slot, :, 0] = key_part.astype(BF16).reshape(NCORE, TOK, DIM)
        parts[slot, :, 1] = value_part.astype(BF16).reshape(NCORE, TOK, DIM)
        return query_grad + jnp.dot(keys.T, slopes, preferred_element_type=F32)

    def backward_group(slots, sem, query_grad):
        for slot in slots:
            query_grad = backward(slot, query_grad)
        for slot in slots:
            push(parts.at[slot, 1 - co], from_core.at[slot], sem, sib, h)
        return query_grad

    def both_cores(slot):
        return parts[slot, co].astype(F32) + from_core[slot].astype(F32)

    def to_y(slots, core_sem, number, sem):
        drain(from_core.at[pl.ds(0, 3)], recv.at[core_sem])
        for step, slot in enumerate(slots):
            y_sum[number, step] = both_cores(slot).astype(BF16)
            push(y_sum.at[number, step], from_y.at[number, step], sem, ctx_at(z, y + step + 1), h)

    beside = [lax.rem(y + step, NY) for step in range(1, NY)]
    virtual = [NY + yy for yy in beside]

    query_grad = jnp.zeros((DIM, ROWS), F32)
    query_grad = backward_group(beside, CP, query_grad)

    drain(acol.at[pl.ds(0, 62)], recv.at[A1])

    def arrange_out(number, carry):
        aperm[2 * number] = acol[owned[number, 0]]
        aperm[2 * number + 1] = acol[owned[number, 1]]
        return carry

    lax.fori_loop(0, N_CTX, arrange_out, 0, unroll=4)

    def deliver_out(step, carry):
        to = lax.rem(c + step, N_CTX)
        push(
            aperm.at[pl.ds(2 * to, 2)], ao.at[:, pl.ds(tile_row, 16), cols(tile_head, DIM)], A2, to, h
        )
        return carry

    lax.fori_loop(1, N_CTX, deliver_out, 0)
    own_out = pltpu.make_async_copy(
        aperm.at[pl.ds(2 * c, 2)], ao.at[:, pl.ds(tile_row, 16), cols(tile_head, DIM)], local.at[LA]
    )
    own_out.start()
    to_y(beside, CP, 0, YP1)

    query_grad = backward_group(virtual, CP + 1, query_grad)
    query_grad = backward_group([y, 2 * NY, own_slot], CP + 2, query_grad)
    to_y(virtual, CP + 1, 1, YPV)

    query_grad = (query_grad * SCALE).astype(BF16)
    for head in range(GROUP):
        dq_rows[:, head * DIM : (head + 1) * DIM] = query_grad[:, head * TOK : (head + 1) * TOK].T
    for step in range(1, N_HEAD):
        to = lax.rem(h + step, N_HEAD)
        push(dq_rows.at[cols(to, PART), :], gq.at[:, cols(h, COLS)], DQ, c, to)
    own_dq = pltpu.make_async_copy(dq_rows.at[cols(h, PART), :], gq.at[:, cols(h, COLS)], local.at[LDQ])
    own_dq.start()

    def home(plane, ctx, first_step):
        for step in range(first_step, N_HEAD):
            to = lax.rem(h + step, N_HEAD)
            push(x_sum.at[plane, :, cols(to, PART), :], from_x.at[plane, h], XP + plane, ctx, to)

    drain(from_core.at[pl.ds(0, 3)], recv.at[CP + 2])
    drain(from_y.at[0], recv.at[YP1])
    before = both_cores(y)
    for step in range(NY - 1):
        before = before + from_y[0, step].astype(F32)
    x_sum[1] = before.astype(BF16)
    home(1, ctx_at(z + 3, y), 0)
    drain(from_y.at[1], recv.at[YPV])
    oldest = both_cores(2 * NY)
    here = both_cores(own_slot)
    for step in range(1, NY):
        sender = lax.rem(y + NY - step, NY)
        piece = from_y[1, step - 1].astype(F32)
        here = here + jnp.where(sender > y, piece, 0.0)
        oldest = oldest + jnp.where(sender > y, 0.0, piece)
    x_sum[0] = oldest.astype(BF16)
    home(0, ctx_at(z + 2, y), 0)
    x_sum[2] = here.astype(BF16)
    home(2, c, 1)
    from_x[2, h] = x_sum[2, :, cols(h, PART), :]

    drain(from_x.at[1], recv.at[XP + 1])
    drain(from_x.at[0], recv.at[XP])
    drain(from_x.at[2, pl.ds(0, 3)], recv.at[XP + 2])
    for head in range(N_HEAD):
        piece = from_x[0, head].astype(F32) + from_x[1, head].astype(F32) + from_x[2, head].astype(F32)
        grads[:, :, head * DIM : (head + 1) * DIM] = piece.astype(BF16)
    own_dk = pltpu.make_async_copy(grads.at[0], gk, local.at[LDK])
    own_dv = pltpu.make_async_copy(grads.at[1], gv, local.at[LDV])
    own_dk.start()
    own_dv.start()

    three_cols = pl.ds(0, 3 * COLS)
    drain(gperm.at[pl.ds(0, 62)], recv.at[A2])
    drain(gq.at[:, three_cols], recv.at[DQ])
    for copy in (own_out, own_dq, own_dk, own_dv):
        copy.wait()
    for sem in (G1, G2, A1, A2):
        drain(gperm.at[pl.ds(0, 62)], send.at[sem])
    for sem in (XQ, DQ):
        drain(gq.at[:, three_cols], send.at[sem])
    for sem in (X0, XP + 2):
        drain(from_x.at[2, pl.ds(0, 3)], send.at[sem])
    for sem in (X1, X2, XP, XP + 1):
        drain(from_x.at[0], send.at[sem])
    for sem in (Y1, YV, YP1, YPV, CP, CP + 1, CP + 2):
        drain(from_y.at[0], send.at[sem])
    drain(kv.at[pl.ds(0, NY), 0], send.at[C1])
    drain(kv.at[pl.ds(0, NY + 1), 0], send.at[CV])


def shards(queries, keys, values, grad_out, owner_lists, doc_lengths):
    hbm = pl.BlockSpec(memory_space=pltpu.HBM)
    smem = pl.BlockSpec(memory_space=pltpu.SMEM)
    block = (2, TOK, DIM)
    piece = (2, PART, DIM)
    ao, gq, gk, gv = pl.pallas_call(
        body,
        out_shape=(
            jax.ShapeDtypeStruct((2, TOK // 2, COLS), BF16),
            jax.ShapeDtypeStruct((PART, N_HEAD * COLS), BF16),
            jax.ShapeDtypeStruct((PART, N_HEAD * DIM), BF16),
            jax.ShapeDtypeStruct((PART, N_HEAD * DIM), BF16),
        ),
        in_specs=[hbm] * 4 + [smem] * 2,
        out_specs=(hbm,) * 4,
        scratch_shapes=[
            pltpu.VMEM((2, PART, N_HEAD * DIM), BF16),
            pltpu.VMEM((SLOTS, NCORE) + block, BF16),
            pltpu.VMEM((TOK, COLS), BF16),
            pltpu.VMEM((2 * N_CTX, 16, DIM), BF16),
            pltpu.VMEM((2 * N_CTX, 16, DIM), BF16),
            pltpu.VMEM((GROUP, 2, TOK // 2, DIM), BF16),
            pltpu.VMEM((2 * N_CTX, 16, DIM), BF16),
            pltpu.VMEM((2 * N_CTX, 16, DIM), BF16),
            pltpu.VMEM((GROUP, 2, TOK // 2, DIM), BF16),
            pltpu.VMEM((TOK, COLS), BF16),
            pltpu.VMEM((ROWS, DIM), BF16),
            pltpu.VMEM((DIM, ROWS), BF16),
            pltpu.VMEM((DIM, ROWS), BF16),
            pltpu.VMEM((SLOTS, PAIR, ROWS), F32),
            pltpu.VMEM((SLOTS, NCORE) + block, BF16),
            pltpu.VMEM((SLOTS,) + block, BF16),
            pltpu.VMEM((2, NY - 1) + block, BF16),
            pltpu.VMEM((2, NY - 1) + block, BF16),
            pltpu.VMEM((PLANES,) + block, BF16),
            pltpu.VMEM((PLANES, N_HEAD) + piece, BF16),
            pltpu.VMEM((2, PART, N_HEAD * DIM), BF16),
            pltpu.VMEM((8, DIM), jnp.int32),
            pltpu.SMEM((8, DIM), jnp.int32),
            pltpu.SemaphoreType.DMA((N_SEM,)),
            pltpu.SemaphoreType.DMA((N_SEM,)),
            pltpu.SemaphoreType.DMA((N_LOCAL,)),
        ],
        compiler_params=pltpu.CompilerParams(
            collective_id=0, has_side_effects=True, vmem_limit_bytes=48 * 1024 * 1024
        ),
        cost_estimate=pl.CostEstimate(flops=4_000_000_000, bytes_accessed=4_000_000, transcendentals=2_300_000),
        name="attention_core",
    )(queries, keys, values, grad_out.reshape(2, TOK // 2, COLS), owner_lists, doc_lengths)
    return ao.reshape(TOK, COLS), gq, gk, gv


def solution(mesh):
    placed = (
        P(("ctx", "head"), None),
        P(("ctx", "head"), None),
        P(("ctx", "head"), None),
        P("ctx", "head"),
        P(),
        P(),
    )
    return jax.shard_map(
        shards,
        mesh=mesh,
        in_specs=placed,
        out_specs=(
            P("ctx", "head"),
            P(("ctx", "head"), None),
            P(("ctx", "head"), None),
            P(("ctx", "head"), None),
        ),
        check_vma=False,
    )
```

```python
import functools
import math

import jax
import jax.numpy as jnp
from jax import lax
from jax.experimental import pallas as pl
from jax.experimental.pallas import tpu as pltpu
from jax.sharding import PartitionSpec as P

MESH = pl.DeviceIdType.MESH
BF16 = jnp.bfloat16
F32 = jnp.float32

N_CTX, N_HEAD = 32, 4
NZ, NY, NCORE = 4, 4, 2
PLANE = NY * NCORE
PLANES = 3
SLOTS = 9
PAIR = 256
TOK = 128
PART = 32
DIM = 128
GROUP = 8
ROWS = TOK * GROUP
COLS = GROUP * DIM
NDOCS = 16
MASKED = -1e30
SCALE = 1.0 / math.sqrt(DIM)
LOG2E = 1.0 / math.log(2.0)

X0, X1, X2, Y1, YV, C1, CV, XQ, G1, G2, A1, A2, DQ, CP, YP1, YPV, XP = *range(14), 16, 17, 18
N_SEM = 21
LK, LV, LRK, LRV, LQ, LG, LA, LDQ, LDK, LDV = range(10)
N_LOCAL = 10


def body(
    q_in, k_in, v_in, go_in, owned, doc_lengths,
    ao, gq, gk, gv,
    raw, kv, qs, gcol, gperm, gos, acol, aperm, out_rows, dq_rows,
    q_rows, q_cols, go_cols, probs, parts, from_core, y_sum, from_y, x_sum, from_x, grads,
    slot_vec, slot_of, send, recv, local,
):
    c = lax.axis_index("ctx")
    h = lax.axis_index("head")
    z = c // PLANE
    idx = lax.rem(c, PLANE)
    y = idx // NCORE
    co = lax.rem(idx, NCORE)
    sib = c + 1 - 2 * co
    tile_row = pl.multiple_of(16 * (c // GROUP), 16)
    tile_head = lax.rem(c, GROUP)

    def ctx_at(zz, yy):
        return lax.rem(zz, NZ) * PLANE + lax.rem(yy, NY) * NCORE + co

    def push(src, dst, sem, ctx, head):
        copy = pltpu.make_async_remote_copy(
            src_ref=src, dst_ref=dst, send_sem=send.at[sem], recv_sem=recv.at[sem],
            device_id=(ctx, head), device_id_type=MESH,
        )
        copy.start()

    def drain(ref, sem):
        pltpu.make_async_copy(ref, ref, sem).wait()

    def cols(number, width):
        return pl.ds(pl.multiple_of(number * width, width), width)

    own_slot = NY + y

    local_copies = [
        pltpu.make_async_copy(k_in.at[:, cols(h, DIM)], kv.at[own_slot, co, 0, cols(h, PART), :], local.at[LK]),
        pltpu.make_async_copy(v_in.at[:, cols(h, DIM)], kv.at[own_slot, co, 1, cols(h, PART), :], local.at[LV]),
        pltpu.make_async_copy(k_in, raw.at[0], local.at[LRK]),
        pltpu.make_async_copy(v_in, raw.at[1], local.at[LRV]),
        pltpu.make_async_copy(q_in.at[:, cols(h, COLS)], qs.at[cols(h, PART), :], local.at[LQ]),
        pltpu.make_async_copy(
            go_in.at[:, pl.ds(tile_row, 16), cols(tile_head, DIM)], gcol.at[pl.ds(2 * c, 2)], local.at[LG]
        ),
    ]
    for copy in local_copies:
        copy.start()

    barrier = pltpu.get_barrier_semaphore()

    def greet(step, carry):
        pl.semaphore_signal(barrier, inc=1, device_id=(lax.rem(c + step, N_CTX), h), device_id_type=MESH)
        return carry

    lax.fori_loop(1, N_CTX, greet, 0)
    for step in range(1, N_HEAD):
        pl.semaphore_signal(barrier, inc=1, device_id=(c, lax.rem(h + step, N_HEAD)), device_id_type=MESH)
        for ahead in (1, 2, 3):
            pl.semaphore_signal(
                barrier, inc=1, device_id=(ctx_at(z + ahead, y), lax.rem(h + step, N_HEAD)), device_id_type=MESH
            )

    lanes = lax.broadcasted_iota(jnp.int32, (8, DIM), 1)
    found = jnp.zeros((8, DIM), jnp.int32)
    for number in range(2 * N_CTX):
        found = jnp.where(lanes == owned[number % 2, number // 2], number, found)
    slot_vec[...] = found
    slot_copy = pltpu.make_async_copy(slot_vec, slot_of, local.at[LA])
    slot_copy.start()

    for copy in local_copies[:4]:
        copy.wait()
    slot_copy.wait()
    pl.semaphore_wait(barrier, N_CTX - 1 + 4 * (N_HEAD - 1))

    def by_head(slot, sem, ctx, first_step):
        for step in range(first_step, N_HEAD):
            to = lax.rem(h + step, N_HEAD)
            push(raw.at[:, :, cols(to, DIM)], kv.at[slot, co, :, cols(h, PART), :], sem, ctx, to)

    by_head(own_slot, X0, c, 1)
    by_head(y, X1, ctx_at(z + 1, y), 0)
    by_head(2 * NY, X2, ctx_at(z + 2, y), 0)
    def tile_of(number):
        return pl.multiple_of(16 * (number // GROUP), 16), lax.rem(number, GROUP)

    def collect_grad(step, carry):
        to = lax.rem(c + step, N_CTX)
        row, head = tile_of(to)
        push(go_in.at[:, pl.ds(row, 16), cols(head, DIM)], gcol.at[pl.ds(2 * c, 2)], G1, to, h)
        return carry

    lax.fori_loop(1, N_CTX, collect_grad, 0)

    for step in range(1, N_HEAD):
        to = lax.rem(h + step, N_HEAD)
        push(q_in.at[:, cols(to, COLS)], qs.at[cols(h, PART), :], XQ, c, to)

    drain(kv.at[0, 0, :, pl.ds(0, 3 * PART), :], recv.at[X0])
    for step in range(1, NY):
        yy = lax.rem(y + step, NY)

        @pl.when(yy > y)
        def _():
            push(kv.at[own_slot, co], kv.at[own_slot, co], YV, ctx_at(z, yy), h)

    drain(kv.at[0, 0], recv.at[X1])
    for step in range(1, NY):
        push(kv.at[y, co], kv.at[y, co], Y1, ctx_at(z, y + step), h)
    drain(kv.at[0, 0], recv.at[X2])
    for step in range(1, NY):
        yy = lax.rem(y + step, NY)

        @pl.when(yy < y)
        def _():
            push(kv.at[2 * NY, co], kv.at[own_slot, co], YV, ctx_at(z, yy), h)

    local_copies[5].wait()
    drain(gcol.at[pl.ds(0, 62)], recv.at[G1])

    def arrange_grad(number, carry):
        gperm[number] = gcol[slot_of[0, number]]
        return carry

    lax.fori_loop(0, 2 * N_CTX, arrange_grad, 0, unroll=8)

    def deliver_grad(step, carry):
        to = lax.rem(c + step, N_CTX)
        push(
            gperm.at[pl.ds(2 * to, 2)], gos.at[tile_head, :, pl.ds(tile_row, 16), :], G2, to, h
        )
        return carry

    lax.fori_loop(1, N_CTX, deliver_grad, 0)
    gos[tile_head, :, pl.ds(tile_row, 16), :] = gperm[pl.ds(2 * c, 2)]

    local_copies[4].wait()
    drain(qs.at[pl.ds(0, 3 * PART), :], recv.at[XQ])
    for head in range(GROUP):
        rows = qs[:, head * DIM : (head + 1) * DIM]
        q_rows[head * TOK : (head + 1) * TOK, :] = rows
        q_cols[:, head * TOK : (head + 1) * TOK] = rows.T

    q_pos = c * TOK + lax.broadcasted_iota(jnp.int32, (1, TOK), 1)
    first = jnp.zeros((1, TOK), jnp.int32)
    begin = jnp.int32(0)
    for doc in range(NDOCS):
        first = jnp.where(q_pos >= begin, jnp.maximum(first, begin), first)
        begin = begin + doc_lengths[doc]

    drain(kv.at[pl.ds(0, 3), 0], recv.at[Y1])
    push(kv.at[pl.ds(0, NY), co], kv.at[pl.ds(0, NY), co], C1, sib, h)
    drain(kv.at[pl.ds(0, 3), 0], recv.at[YV])
    push(kv.at[pl.ds(NY, NY + 1), co], kv.at[pl.ds(NY, NY + 1), co], CV, sib, h)

    def position(slot):
        if slot < NY:
            return ((z - 1) * NY + slot) * PAIR
        if slot < 2 * NY:
            return (jnp.where(slot - NY <= y, z, z - 2) * NY + slot - NY) * PAIR
        return ((z - 2) * NY + y) * PAIR

    def scores(slot, peak):
        keys = kv[slot, :, 0].reshape(PAIR, DIM)
        key_pos = position(slot) + lax.broadcasted_iota(jnp.int32, (PAIR, TOK), 0)
        bias = jnp.where((key_pos <= q_pos) & (key_pos >= first), 0.0, MASKED)
        bias = jnp.concatenate([bias] * GROUP, axis=1)
        block = jnp.dot(keys, q_cols[...], preferred_element_type=F32) * (SCALE * LOG2E) + bias
        probs[slot] = block
        return jnp.maximum(peak, jnp.max(block.reshape(PAIR // 8, 8, ROWS), axis=0))

    peak = jnp.full((8, ROWS), MASKED, F32)
    drain(kv.at[pl.ds(0, NY), 0], recv.at[C1])
    for slot in range(NY):
        peak = scores(slot, peak)
    drain(kv.at[pl.ds(0, NY + 1), 0], recv.at[CV])
    for slot in range(NY, SLOTS):
        peak = scores(slot, peak)
    peak = jnp.max(peak, axis=0, keepdims=True)

    total = jnp.zeros((8, ROWS), F32)
    accum = jnp.zeros((DIM, ROWS), F32)
    for slot in range(SLOTS):
        values = kv[slot, :, 1].reshape(PAIR, DIM)
        block = jnp.exp2(probs[slot] - peak)
        probs[slot] = block
        total = total + jnp.sum(block.reshape(PAIR // 8, 8, ROWS), axis=0)
        accum = accum + jnp.dot(values.T, block.astype(BF16), preferred_element_type=F32)
    inverse = 1.0 / jnp.sum(total, axis=0, keepdims=True)
    rounded = (accum * inverse).astype(BF16)
    for head in range(GROUP):
        rows = rounded[:, head * TOK : (head + 1) * TOK].T
        out_rows[head, 0] = rows[:64]
        out_rows[head, 1] = rows[64:]

    def collect_out(step, carry):
        to = lax.rem(c + step, N_CTX)
        row, head = tile_of(to)
        push(out_rows.at[head, :, pl.ds(row, 16), :], acol.at[pl.ds(2 * c, 2)], A1, to, h)
        return carry

    lax.fori_loop(1, N_CTX, collect_out, 0)
    acol[pl.ds(2 * c, 2)] = out_rows[tile_head, :, pl.ds(tile_row, 16), :]

    drain(gperm.at[pl.ds(0, 62)], recv.at[G2])
    for head in range(GROUP):
        go_cols[:, head * TOK : (head + 1) * TOK] = gos[head].reshape(TOK, DIM).T
    delta = jnp.sum(go_cols[...].astype(F32) * rounded.astype(F32), axis=0, keepdims=True)

    def backward(slot, query_grad):
        keys, values = kv[slot, :, 0].reshape(PAIR, DIM), kv[slot, :, 1].reshape(PAIR, DIM)
        weights = probs[slot] * inverse
        pushed = jnp.dot(values, go_cols[...], preferred_element_type=F32)
        slopes = (weights * (pushed - delta)).astype(BF16)
        go_rows = gos[...].reshape(ROWS, DIM)
        key_part = jnp.dot(slopes, q_rows[...], preferred_element_type=F32) * SCALE
        value_part = jnp.dot(weights.astype(BF16), go_rows, preferred_element_type=F32)
        parts[slot, :, 0] = key_part.astype(BF16).reshape(NCORE, TOK, DIM)
        parts[slot, :, 1] = value_part.astype(BF16).reshape(NCORE, TOK, DIM)
        return query_grad + jnp.dot(keys.T, slopes, preferred_element_type=F32)

    def backward_group(slots, sem, query_grad):
        for slot in slots:
            query_grad = backward(slot, query_grad)
        for slot in slots:
            push(parts.at[slot, 1 - co], from_core.at[slot], sem, sib, h)
        return query_grad

    def both_cores(slot):
        return parts[slot, co].astype(F32) + from_core[slot].astype(F32)

    def to_y(slots, core_sem, number, sem):
        drain(from_core.at[pl.ds(0, 3)], recv.at[core_sem])
        for step, slot in enumerate(slots):
            y_sum[number, step] = both_cores(slot).astype(BF16)
            push(y_sum.at[number, step], from_y.at[number, step], sem, ctx_at(z, y + step + 1), h)

    beside = [lax.rem(y + step, NY) for step in range(1, NY)]
    virtual = [NY + yy for yy in beside]

    query_grad = jnp.zeros((DIM, ROWS), F32)
    query_grad = backward_group(beside, CP, query_grad)

    query_grad = backward_group(virtual, CP + 1, query_grad)
    to_y(beside, CP, 0, YP1)
    query_grad = backward_group([y, 2 * NY, own_slot], CP + 2, query_grad)
    to_y(virtual, CP + 1, 1, YPV)

    query_grad = (query_grad * SCALE).astype(BF16)
    for head in range(GROUP):
        dq_rows[:, head * DIM : (head + 1) * DIM] = query_grad[:, head * TOK : (head + 1) * TOK].T
    for step in range(1, N_HEAD):
        to = lax.rem(h + step, N_HEAD)
        push(dq_rows.at[cols(to, PART), :], gq.at[:, cols(h, COLS)], DQ, c, to)
    own_dq = pltpu.make_async_copy(dq_rows.at[cols(h, PART), :], gq.at[:, cols(h, COLS)], local.at[LDQ])
    own_dq.start()

    drain(acol.at[pl.ds(0, 62)], recv.at[A1])

    def arrange_out(number, carry):
        aperm[2 * number] = acol[owned[0, number]]
        aperm[2 * number + 1] = acol[owned[1, number]]
        return carry

    lax.fori_loop(0, N_CTX, arrange_out, 0, unroll=4)

    def deliver_out(step, carry):
        to = lax.rem(c + step, N_CTX)
        push(
            aperm.at[pl.ds(2 * to, 2)], ao.at[:, pl.ds(tile_row, 16), cols(tile_head, DIM)], A2, to, h
        )
        return carry

    lax.fori_loop(1, N_CTX, deliver_out, 0)
    own_out = pltpu.make_async_copy(
        aperm.at[pl.ds(2 * c, 2)], ao.at[:, pl.ds(tile_row, 16), cols(tile_head, DIM)], local.at[LA]
    )
    own_out.start()
    def home(plane, ctx, first_step):
        for step in range(first_step, N_HEAD):
            to = lax.rem(h + step, N_HEAD)
            push(x_sum.at[plane, :, cols(to, PART), :], from_x.at[plane, h], XP + plane, ctx, to)

    drain(from_core.at[pl.ds(0, 3)], recv.at[CP + 2])
    drain(from_y.at[0], recv.at[YP1])
    before = both_cores(y)
    for step in range(NY - 1):
        before = before + from_y[0, step].astype(F32)
    x_sum[1] = before.astype(BF16)
    home(1, ctx_at(z + 3, y), 0)
    drain(from_y.at[1], recv.at[YPV])
    oldest = both_cores(2 * NY)
    here = both_cores(own_slot)
    for step in range(1, NY):
        sender = lax.rem(y + NY - step, NY)
        piece = from_y[1, step - 1].astype(F32)
        here = here + jnp.where(sender > y, piece, 0.0)
        oldest = oldest + jnp.where(sender > y, 0.0, piece)
    x_sum[0] = oldest.astype(BF16)
    home(0, ctx_at(z + 2, y), 0)
    x_sum[2] = here.astype(BF16)
    home(2, c, 1)
    from_x[2, h] = x_sum[2, :, cols(h, PART), :]

    drain(from_x.at[1], recv.at[XP + 1])
    drain(from_x.at[0], recv.at[XP])
    drain(from_x.at[2, pl.ds(0, 3)], recv.at[XP + 2])
    for head in range(N_HEAD):
        piece = from_x[0, head].astype(F32) + from_x[1, head].astype(F32) + from_x[2, head].astype(F32)
        grads[:, :, head * DIM : (head + 1) * DIM] = piece.astype(BF16)
    own_dk = pltpu.make_async_copy(grads.at[0], gk, local.at[LDK])
    own_dv = pltpu.make_async_copy(grads.at[1], gv, local.at[LDV])
    own_dk.start()
    own_dv.start()

    three_cols = pl.ds(0, 3 * COLS)
    drain(gperm.at[pl.ds(0, 62)], recv.at[A2])
    drain(gq.at[:, three_cols], recv.at[DQ])
    for copy in (own_out, own_dq, own_dk, own_dv):
        copy.wait()
    for sem in (G1, G2, A1, A2):
        drain(gperm.at[pl.ds(0, 62)], send.at[sem])
    for sem in (XQ, DQ):
        drain(gq.at[:, three_cols], send.at[sem])
    for sem in (X0, XP + 2):
        drain(from_x.at[2, pl.ds(0, 3)], send.at[sem])
    for sem in (X1, X2, XP, XP + 1):
        drain(from_x.at[0], send.at[sem])
    for sem in (Y1, YV, YP1, YPV, CP, CP + 1, CP + 2):
        drain(from_y.at[0], send.at[sem])
    drain(kv.at[pl.ds(0, NY), 0], send.at[C1])
    drain(kv.at[pl.ds(0, NY + 1), 0], send.at[CV])


def finish_body(ao, gq, gk, gv, ao_out, gq_out, gk_out, gv_out, sems):
    copies = [
        pltpu.make_async_copy(src, dst, sems.at[number])
        for number, (src, dst) in enumerate(((ao, ao_out), (gq, gq_out), (gk, gk_out), (gv, gv_out)))
    ]
    for copy in copies:
        copy.start()
    for copy in copies:
        copy.wait()


def finish(*arrays):
    anywhere = pl.BlockSpec(memory_space=pltpu.VMEM)
    hbm = pl.BlockSpec(memory_space=pltpu.HBM)
    return pl.pallas_call(
        finish_body,
        out_shape=tuple(jax.ShapeDtypeStruct(array.shape, array.dtype) for array in arrays),
        in_specs=[anywhere] * 4,
        out_specs=(hbm,) * 4,
        scratch_shapes=[pltpu.SemaphoreType.DMA((4,))],
        name="write_outputs",
    )(*arrays)


def shards(queries, keys, values, grad_out, owner_lists, doc_lengths):
    hbm = pl.BlockSpec(memory_space=pltpu.HBM)
    smem = pl.BlockSpec(memory_space=pltpu.SMEM)
    block = (2, TOK, DIM)
    piece = (2, PART, DIM)
    ao, gq, gk, gv = pl.pallas_call(
        body,
        out_shape=(
            jax.ShapeDtypeStruct((2, TOK // 2, COLS), BF16),
            jax.ShapeDtypeStruct((PART, N_HEAD * COLS), BF16),
            jax.ShapeDtypeStruct((PART, N_HEAD * DIM), BF16),
            jax.ShapeDtypeStruct((PART, N_HEAD * DIM), BF16),
        ),
        in_specs=[hbm] * 4 + [smem] * 2,
        out_specs=(hbm,) * 4,
        scratch_shapes=[
            pltpu.VMEM((2, PART, N_HEAD * DIM), BF16),
            pltpu.VMEM((SLOTS, NCORE) + block, BF16),
            pltpu.VMEM((TOK, COLS), BF16),
            pltpu.VMEM((2 * N_CTX, 16, DIM), BF16),
            pltpu.VMEM((2 * N_CTX, 16, DIM), BF16),
            pltpu.VMEM((GROUP, 2, TOK // 2, DIM), BF16),
            pltpu.VMEM((2 * N_CTX, 16, DIM), BF16),
            pltpu.VMEM((2 * N_CTX, 16, DIM), BF16),
            pltpu.VMEM((GROUP, 2, TOK // 2, DIM), BF16),
            pltpu.VMEM((TOK, COLS), BF16),
            pltpu.VMEM((ROWS, DIM), BF16),
            pltpu.VMEM((DIM, ROWS), BF16),
            pltpu.VMEM((DIM, ROWS), BF16),
            pltpu.VMEM((SLOTS, PAIR, ROWS), F32),
            pltpu.VMEM((SLOTS, NCORE) + block, BF16),
            pltpu.VMEM((SLOTS,) + block, BF16),
            pltpu.VMEM((2, NY - 1) + block, BF16),
            pltpu.VMEM((2, NY - 1) + block, BF16),
            pltpu.VMEM((PLANES,) + block, BF16),
            pltpu.VMEM((PLANES, N_HEAD) + piece, BF16),
            pltpu.VMEM((2, PART, N_HEAD * DIM), BF16),
            pltpu.VMEM((8, DIM), jnp.int32),
            pltpu.SMEM((8, DIM), jnp.int32),
            pltpu.SemaphoreType.DMA((N_SEM,)),
            pltpu.SemaphoreType.DMA((N_SEM,)),
            pltpu.SemaphoreType.DMA((N_LOCAL,)),
        ],
        compiler_params=pltpu.CompilerParams(
            collective_id=0, has_side_effects=True, vmem_limit_bytes=56 * 1024 * 1024
        ),
        cost_estimate=pl.CostEstimate(flops=4_000_000_000, bytes_accessed=4_000_000, transcendentals=2_300_000),
        name="attention_core",
    )(queries, keys, values, grad_out.reshape(2, TOK // 2, COLS), owner_lists.T, doc_lengths)
    return finish(ao.reshape(TOK, COLS), gq, gk, gv)


def solution(mesh):
    placed = (
        P(("ctx", "head"), None),
        P(("ctx", "head"), None),
        P(("ctx", "head"), None),
        P("ctx", "head"),
        P(),
        P(),
    )
    return jax.shard_map(
        shards,
        mesh=mesh,
        in_specs=placed,
        out_specs=(
            P("ctx", "head"),
            P(("ctx", "head"), None),
            P(("ctx", "head"), None),
            P(("ctx", "head"), None),
        ),
        check_vma=False,
    )
```

```python
import functools
import math

import jax
import jax.numpy as jnp
from jax import lax
from jax.experimental import pallas as pl
from jax.experimental.pallas import tpu as pltpu
from jax.sharding import PartitionSpec as P

MESH = pl.DeviceIdType.MESH
BF16 = jnp.bfloat16
F32 = jnp.float32

N_CTX, N_HEAD = 32, 4
NZ, NY, NCORE = 4, 4, 2
PLANE = NY * NCORE
PLANES = 3
SLOTS = 9
PAIR = 256
TOK = 128
PART = 32
DIM = 128
GROUP = 8
ROWS = TOK * GROUP
COLS = GROUP * DIM
NDOCS = 16
MASKED = -1e30
SCALE = 1.0 / math.sqrt(DIM)
LOG2E = 1.0 / math.log(2.0)

XQ, G1, G2, A1, A2, DQ = range(6)
X0, X1, X2, Y1, YV, C1, CV, YP, XPV, XP, CP = (6, 8, 10, 12, 14, 16, 18, 20, 22, 24, 30)
N_SEM = 36
LK, LV, LRK, LRV, LQ, LG, LA, LDQ, LDK, LDV = range(10)
N_LOCAL = 10


def body(
    q_in, k_in, v_in, go_in, owned, doc_lengths,
    ao, gq, gk, gv,
    raw, kv, qs, gcol, gperm, gos, acol, aperm, out_rows, dq_rows,
    q_rows, q_cols, go_cols, probs, rounded_probs, parts, from_core, y_sum, from_y, sums, from_x, grads,
    slot_vec, slot_of, send, recv, local,
):
    c = lax.axis_index("ctx")
    h = lax.axis_index("head")
    z = c // PLANE
    idx = lax.rem(c, PLANE)
    y = idx // NCORE
    co = lax.rem(idx, NCORE)
    sib = c + 1 - 2 * co
    tile_row = pl.multiple_of(16 * (c // GROUP), 16)
    tile_head = lax.rem(c, GROUP)

    def ctx_at(zz, yy):
        return lax.rem(zz, NZ) * PLANE + lax.rem(yy, NY) * NCORE + co

    def push(src, dst, sem, ctx, head):
        copy = pltpu.make_async_remote_copy(
            src_ref=src, dst_ref=dst, send_sem=send.at[sem], recv_sem=recv.at[sem],
            device_id=(ctx, head), device_id_type=MESH,
        )
        copy.start()

    def drain(ref, sem):
        pltpu.make_async_copy(ref, ref, sem).wait()

    def cols(number, width):
        return pl.ds(pl.multiple_of(number * width, width), width)

    own_slot = NY + y

    local_copies = [
        pltpu.make_async_copy(k_in.at[:, cols(h, DIM)], kv.at[0, own_slot, co, cols(h, PART), :], local.at[LK]),
        pltpu.make_async_copy(v_in.at[:, cols(h, DIM)], kv.at[1, own_slot, co, cols(h, PART), :], local.at[LV]),
        pltpu.make_async_copy(k_in, raw.at[0], local.at[LRK]),
        pltpu.make_async_copy(v_in, raw.at[1], local.at[LRV]),
        pltpu.make_async_copy(q_in.at[:, cols(h, COLS)], qs.at[cols(h, PART), :], local.at[LQ]),
        pltpu.make_async_copy(
            go_in.at[:, pl.ds(tile_row, 16), cols(tile_head, DIM)], gcol.at[pl.ds(2 * c, 2)], local.at[LG]
        ),
    ]
    for copy in local_copies:
        copy.start()

    barrier = pltpu.get_barrier_semaphore()

    def greet(step, carry):
        pl.semaphore_signal(barrier, inc=1, device_id=(lax.rem(c + step, N_CTX), h), device_id_type=MESH)
        return carry

    lax.fori_loop(1, N_CTX, greet, 0)
    def greet_heads(ctx):
        for step in range(1, N_HEAD):
            pl.semaphore_signal(barrier, inc=1, device_id=(ctx, lax.rem(h + step, N_HEAD)), device_id_type=MESH)

    for ahead in range(NZ):
        greet_heads(ctx_at(z + ahead, y))
    for step in range(1, NY):
        greet_heads(ctx_at(z, y + step))
        greet_heads(ctx_at(z + 2, y + step))

    lanes = lax.broadcasted_iota(jnp.int32, (8, DIM), 1)
    found = jnp.zeros((8, DIM), jnp.int32)
    for number in range(2 * N_CTX):
        found = jnp.where(lanes == owned[number % 2, number // 2], number, found)
    slot_vec[...] = found
    slot_copy = pltpu.make_async_copy(slot_vec, slot_of, local.at[LA])
    slot_copy.start()

    for copy in local_copies[:4]:
        copy.wait()
    slot_copy.wait()
    pl.semaphore_wait(barrier, N_CTX - 1 + (NZ + 2 * (NY - 1)) * (N_HEAD - 1))

    def tile_of(number):
        return pl.multiple_of(16 * (number // GROUP), 16), lax.rem(number, GROUP)

    def collect_grad(step, carry):
        to = lax.rem(c + step, N_CTX)
        row, head = tile_of(to)
        push(go_in.at[:, pl.ds(row, 16), cols(head, DIM)], gcol.at[pl.ds(2 * c, 2)], G1, to, h)
        return carry

    lax.fori_loop(1, N_CTX, collect_grad, 0)

    def by_head(which, slot, sem, ctx, first_step):
        for step in range(first_step, N_HEAD):
            to = lax.rem(h + step, N_HEAD)
            push(
                raw.at[which, :, cols(to, DIM)], kv.at[which, slot, co, cols(h, PART), :], sem + which, ctx, to
            )

    def first_hop(which):
        by_head(which, y, X1, ctx_at(z + 1, y), 0)
        by_head(which, 2 * NY, X2, ctx_at(z + 2, y), 0)
        by_head(which, own_slot, X0, c, 1)
        for step in range(1, NY):
            yy = lax.rem(y + step, NY)

            @pl.when(yy > y)
            def _():
                by_head(which, own_slot, YV, ctx_at(z, yy), 0)

    first_hop(0)
    for step in range(1, N_HEAD):
        to = lax.rem(h + step, N_HEAD)
        push(q_in.at[:, cols(to, COLS)], qs.at[cols(h, PART), :], XQ, c, to)
    first_hop(1)

    def along_y(which):
        drain(kv.at[0, 0, 0], recv.at[X1 + which])
        for step in range(1, NY):
            push(kv.at[which, y, co], kv.at[which, y, co], Y1 + which, ctx_at(z, y + step), h)
        drain(kv.at[0, 0, 0], recv.at[X2 + which])
        for step in range(1, NY):
            yy = lax.rem(y + step, NY)

            @pl.when(yy < y)
            def _():
                push(kv.at[which, 2 * NY, co], kv.at[which, own_slot, co], YV + which, ctx_at(z, yy), h)

    along_y(0)
    along_y(1)

    q_pos = c * TOK + lax.broadcasted_iota(jnp.int32, (1, TOK), 1)
    first = jnp.zeros((1, TOK), jnp.int32)
    begin = jnp.int32(0)
    for doc in range(NDOCS):
        first = jnp.where(q_pos >= begin, jnp.maximum(first, begin), first)
        begin = begin + doc_lengths[doc]

    local_copies[5].wait()
    drain(gcol.at[pl.ds(0, 62)], recv.at[G1])

    def arrange_grad(number, carry):
        gperm[number] = gcol[slot_of[0, number]]
        return carry

    lax.fori_loop(0, 2 * N_CTX, arrange_grad, 0, unroll=8)

    def deliver_grad(step, carry):
        to = lax.rem(c + step, N_CTX)
        push(
            gperm.at[pl.ds(2 * to, 2)], gos.at[tile_head, :, pl.ds(tile_row, 16), :], G2, to, h
        )
        return carry

    lax.fori_loop(1, N_CTX, deliver_grad, 0)
    gos[tile_head, :, pl.ds(tile_row, 16), :] = gperm[pl.ds(2 * c, 2)]

    local_copies[4].wait()
    drain(qs.at[pl.ds(0, 3 * PART), :], recv.at[XQ])
    for head in range(GROUP):
        rows = qs[:, head * DIM : (head + 1) * DIM]
        q_rows[head * TOK : (head + 1) * TOK, :] = rows
        q_cols[:, head * TOK : (head + 1) * TOK] = rows.T

    def to_other_core(which):
        drain(kv.at[0, pl.ds(0, 3), 0], recv.at[Y1 + which])
        push(kv.at[which, pl.ds(0, NY), co], kv.at[which, pl.ds(0, NY), co], C1 + which, sib, h)
        drain(kv.at[0, 0, 0, pl.ds(0, 3 * PART), :], recv.at[X0 + which])
        drain(kv.at[0, pl.ds(0, 3), 0], recv.at[YV + which])
        push(kv.at[which, pl.ds(NY, NY + 1), co], kv.at[which, pl.ds(NY, NY + 1), co], CV + which, sib, h)

    to_other_core(0)

    def position(slot):
        if slot < NY:
            return ((z - 1) * NY + slot) * PAIR
        if slot < 2 * NY:
            return (jnp.where(slot - NY <= y, z, z - 2) * NY + slot - NY) * PAIR
        return ((z - 2) * NY + y) * PAIR

    def scores(slot, peak):
        keys = kv[0, slot].reshape(PAIR, DIM)
        key_pos = position(slot) + lax.broadcasted_iota(jnp.int32, (PAIR, TOK), 0)
        bias = jnp.where((key_pos <= q_pos) & (key_pos >= first), 0.0, MASKED)
        bias = jnp.concatenate([bias] * GROUP, axis=1)
        block = jnp.dot(keys, q_cols[...], preferred_element_type=F32) * (SCALE * LOG2E) + bias
        probs[slot] = block
        return jnp.maximum(peak, jnp.max(block.reshape(PAIR // 8, 8, ROWS), axis=0))

    peak = jnp.full((8, ROWS), MASKED, F32)
    drain(kv.at[0, pl.ds(0, NY), 0], recv.at[C1])
    for slot in range(NY):
        peak = scores(slot, peak)
    drain(kv.at[0, pl.ds(0, NY + 1), 0], recv.at[CV])
    for slot in range(NY, SLOTS):
        peak = scores(slot, peak)
    peak = jnp.max(peak, axis=0, keepdims=True)
    to_other_core(1)

    total = jnp.zeros((8, ROWS), F32)
    for slot in range(SLOTS):
        block = jnp.exp2(probs[slot] - peak)
        probs[slot] = block
        rounded_probs[slot] = block.astype(BF16)
        total = total + jnp.sum(block.reshape(PAIR // 8, 8, ROWS), axis=0)
    drain(kv.at[0, pl.ds(0, NY), 0], recv.at[C1 + 1])
    drain(kv.at[0, pl.ds(0, NY + 1), 0], recv.at[CV + 1])
    accum = jnp.zeros((DIM, ROWS), F32)
    for slot in range(SLOTS):
        values = kv[1, slot].reshape(PAIR, DIM)
        accum = accum + jnp.dot(values.T, rounded_probs[slot], preferred_element_type=F32)
    inverse = 1.0 / jnp.sum(total, axis=0, keepdims=True)
    rounded = (accum * inverse).astype(BF16)
    for head in range(GROUP):
        rows = rounded[:, head * TOK : (head + 1) * TOK].T
        out_rows[head, 0] = rows[:64]
        out_rows[head, 1] = rows[64:]

    def collect_out(step, carry):
        to = lax.rem(c + step, N_CTX)
        row, head = tile_of(to)
        push(out_rows.at[head, :, pl.ds(row, 16), :], acol.at[pl.ds(2 * c, 2)], A1, to, h)
        return carry

    lax.fori_loop(1, N_CTX, collect_out, 0)
    acol[pl.ds(2 * c, 2)] = out_rows[tile_head, :, pl.ds(tile_row, 16), :]

    drain(gperm.at[pl.ds(0, 62)], recv.at[G2])
    for head in range(GROUP):
        go_cols[:, head * TOK : (head + 1) * TOK] = gos[head].reshape(TOK, DIM).T
    delta = jnp.sum(go_cols[...].astype(F32) * rounded.astype(F32), axis=0, keepdims=True)

    beside = [lax.rem(y + step, NY) for step in range(1, NY)]
    virtual = [NY + yy for yy in beside]
    rest = [y, 2 * NY, own_slot]

    def both_cores(which, slot):
        return parts[which, slot, co].astype(F32) + from_core[which, slot].astype(F32)

    def home(which, number, sem, ctx, first_step):
        for step in range(first_step, N_HEAD):
            to = lax.rem(h + step, N_HEAD)
            push(sums.at[which, number, cols(to, PART), :], from_x.at[which, number, h], sem, ctx, to)

    def beside_home(which):
        for step, slot in enumerate(beside):
            y_sum[which, step] = both_cores(which, slot).astype(BF16)
            push(y_sum.at[which, step], from_y.at[which, step], YP + which, ctx_at(z, y + step + 1), h)

    def virtual_home(which):
        for step, slot in enumerate(virtual):
            sums[which, PLANES + step] = both_cores(which, slot).astype(BF16)
            plane = jnp.where(beside[step] <= y, z, z + 2)
            home(which, PLANES + step, XPV + which, ctx_at(plane, beside[step]), 0)

    def rest_home(which):
        sums[which, 0] = both_cores(which, 2 * NY).astype(BF16)
        home(which, 0, XP + 3 * which, ctx_at(z + 2, y), 0)
        sums[which, 2] = both_cores(which, own_slot).astype(BF16)
        home(which, 2, XP + 3 * which + 2, c, 1)
        from_x[which, 2, h] = sums[which, 2, cols(h, PART), :]

    def before_home(which):
        drain(from_y.at[0], recv.at[YP + which])
        before = both_cores(which, y)
        for step in range(NY - 1):
            before = before + from_y[which, step].astype(F32)
        sums[which, 1] = before.astype(BF16)
        home(which, 1, XP + 3 * which + 1, ctx_at(z + 3, y), 0)

    def value_group(slots, sem):
        for slot in slots:
            weights = (probs[slot] * inverse).astype(BF16)
            part = jnp.dot(weights, gos[...].reshape(ROWS, DIM), preferred_element_type=F32)
            parts[1, slot] = part.astype(BF16).reshape(NCORE, TOK, DIM)
        for slot in slots:
            push(parts.at[1, slot, 1 - co], from_core.at[1, slot], sem, sib, h)

    def key_group(slots, sem, query_grad):
        for slot in slots:
            keys, values = kv[0, slot].reshape(PAIR, DIM), kv[1, slot].reshape(PAIR, DIM)
            pushed = jnp.dot(values, go_cols[...], preferred_element_type=F32)
            slopes = (probs[slot] * inverse * (pushed - delta)).astype(BF16)
            part = jnp.dot(slopes, q_rows[...], preferred_element_type=F32) * SCALE
            parts[0, slot] = part.astype(BF16).reshape(NCORE, TOK, DIM)
            query_grad = query_grad + jnp.dot(keys.T, slopes, preferred_element_type=F32)
        for slot in slots:
            push(parts.at[0, slot, 1 - co], from_core.at[0, slot], sem, sib, h)
        return query_grad

    def drain_core(sem):
        drain(from_core.at[0, pl.ds(0, 3)], recv.at[sem])

    value_group(beside, CP)
    value_group(virtual, CP + 1)
    value_group(rest, CP + 2)
    query_grad = jnp.zeros((DIM, ROWS), F32)
    query_grad = key_group(beside, CP + 3, query_grad)
    drain_core(CP)
    beside_home(1)
    drain_core(CP + 1)
    virtual_home(1)
    drain_core(CP + 2)
    rest_home(1)
    query_grad = key_group(virtual, CP + 4, query_grad)
    drain_core(CP + 3)
    beside_home(0)
    query_grad = key_group(rest, CP + 5, query_grad)
    drain_core(CP + 4)
    virtual_home(0)

    query_grad = (query_grad * SCALE).astype(BF16)
    for head in range(GROUP):
        dq_rows[:, head * DIM : (head + 1) * DIM] = query_grad[:, head * TOK : (head + 1) * TOK].T
    for step in range(1, N_HEAD):
        to = lax.rem(h + step, N_HEAD)
        push(dq_rows.at[cols(to, PART), :], gq.at[:, cols(h, COLS)], DQ, c, to)
    own_dq = pltpu.make_async_copy(dq_rows.at[cols(h, PART), :], gq.at[:, cols(h, COLS)], local.at[LDQ])
    own_dq.start()

    drain(acol.at[pl.ds(0, 62)], recv.at[A1])

    def arrange_out(number, carry):
        aperm[2 * number] = acol[owned[0, number]]
        aperm[2 * number + 1] = acol[owned[1, number]]
        return carry

    lax.fori_loop(0, N_CTX, arrange_out, 0, unroll=4)

    def deliver_out(step, carry):
        to = lax.rem(c + step, N_CTX)
        push(
            aperm.at[pl.ds(2 * to, 2)], ao.at[:, pl.ds(tile_row, 16), cols(tile_head, DIM)], A2, to, h
        )
        return carry

    lax.fori_loop(1, N_CTX, deliver_out, 0)
    own_out = pltpu.make_async_copy(
        aperm.at[pl.ds(2 * c, 2)], ao.at[:, pl.ds(tile_row, 16), cols(tile_head, DIM)], local.at[LA]
    )
    own_out.start()
    drain_core(CP + 5)
    rest_home(0)
    before_home(1)
    before_home(0)

    for which in (1, 0):
        drain(from_x.at[0, pl.ds(PLANES, 3)], recv.at[XPV + which])
        drain(from_x.at[0, 0], recv.at[XP + 3 * which])
        drain(from_x.at[0, 0, pl.ds(0, 3)], recv.at[XP + 3 * which + 2])
        drain(from_x.at[0, 0], recv.at[XP + 3 * which + 1])
        for head in range(N_HEAD):
            piece = from_x[which, 0, head].astype(F32)
            for number in range(1, PLANES + NY - 1):
                piece = piece + from_x[which, number, head].astype(F32)
            grads[which, :, head * DIM : (head + 1) * DIM] = piece.astype(BF16)
    own_dk = pltpu.make_async_copy(grads.at[0], gk, local.at[LDK])
    own_dv = pltpu.make_async_copy(grads.at[1], gv, local.at[LDV])
    own_dk.start()
    own_dv.start()

    three_cols = pl.ds(0, 3 * COLS)
    drain(gperm.at[pl.ds(0, 62)], recv.at[A2])
    drain(gq.at[:, three_cols], recv.at[DQ])
    for copy in (own_out, own_dq, own_dk, own_dv):
        copy.wait()
    for sem in (G1, G2, A1, A2):
        drain(gperm.at[pl.ds(0, 62)], send.at[sem])
    for sem in (XQ, DQ):
        drain(gq.at[:, three_cols], send.at[sem])
    for which in range(2):
        for sem in (X0 + which, XP + 3 * which + 2):
            drain(from_x.at[0, 0, pl.ds(0, 3)], send.at[sem])
        for sem in (X1 + which, X2 + which, XP + 3 * which, XP + 3 * which + 1):
            drain(from_x.at[0, 0], send.at[sem])
        for sem in (Y1, YV, YP, XPV):
            drain(from_y.at[0], send.at[sem + which])
        for sem in range(3):
            drain(from_y.at[0], send.at[CP + 3 * which + sem])
        drain(kv.at[0, pl.ds(0, NY), 0], send.at[C1 + which])
        drain(kv.at[0, pl.ds(0, NY + 1), 0], send.at[CV + which])


def finish_body(ao, gq, gk, gv, ao_out, gq_out, gk_out, gv_out, sems):
    copies = [
        pltpu.make_async_copy(src, dst, sems.at[number])
        for number, (src, dst) in enumerate(((ao, ao_out), (gq, gq_out), (gk, gk_out), (gv, gv_out)))
    ]
    for copy in copies:
        copy.start()
    for copy in copies:
        copy.wait()


def finish(*arrays):
    anywhere = pl.BlockSpec(memory_space=pltpu.VMEM)
    hbm = pl.BlockSpec(memory_space=pltpu.HBM)
    return pl.pallas_call(
        finish_body,
        out_shape=tuple(jax.ShapeDtypeStruct(array.shape, array.dtype) for array in arrays),
        in_specs=[anywhere] * 4,
        out_specs=(hbm,) * 4,
        scratch_shapes=[pltpu.SemaphoreType.DMA((4,))],
        name="write_outputs",
    )(*arrays)


def shards(queries, keys, values, grad_out, owner_lists, doc_lengths):
    hbm = pl.BlockSpec(memory_space=pltpu.HBM)
    smem = pl.BlockSpec(memory_space=pltpu.SMEM)
    block = (TOK, DIM)
    ao, gq, gk, gv = pl.pallas_call(
        body,
        out_shape=(
            jax.ShapeDtypeStruct((2, TOK // 2, COLS), BF16),
            jax.ShapeDtypeStruct((PART, N_HEAD * COLS), BF16),
            jax.ShapeDtypeStruct((PART, N_HEAD * DIM), BF16),
            jax.ShapeDtypeStruct((PART, N_HEAD * DIM), BF16),
        ),
        in_specs=[hbm] * 4 + [smem] * 2,
        out_specs=(hbm,) * 4,
        scratch_shapes=[
            pltpu.VMEM((2, PART, N_HEAD * DIM), BF16),
            pltpu.VMEM((2, SLOTS, NCORE) + block, BF16),
            pltpu.VMEM((TOK, COLS), BF16),
            pltpu.VMEM((2 * N_CTX, 16, DIM), BF16),
            pltpu.VMEM((2 * N_CTX, 16, DIM), BF16),
            pltpu.VMEM((GROUP, 2, TOK // 2, DIM), BF16),
            pltpu.VMEM((2 * N_CTX, 16, DIM), BF16),
            pltpu.VMEM((2 * N_CTX, 16, DIM), BF16),
            pltpu.VMEM((GROUP, 2, TOK // 2, DIM), BF16),
            pltpu.VMEM((TOK, COLS), BF16),
            pltpu.VMEM((ROWS, DIM), BF16),
            pltpu.VMEM((DIM, ROWS), BF16),
            pltpu.VMEM((DIM, ROWS), BF16),
            pltpu.VMEM((SLOTS, PAIR, ROWS), F32),
            pltpu.VMEM((SLOTS, PAIR, ROWS), BF16),
            pltpu.VMEM((2, SLOTS, NCORE) + block, BF16),
            pltpu.VMEM((2, SLOTS) + block, BF16),
            pltpu.VMEM((2, NY - 1) + block, BF16),
            pltpu.VMEM((2, NY - 1) + block, BF16),
            pltpu.VMEM((2, PLANES + NY - 1) + block, BF16),
            pltpu.VMEM((2, PLANES + NY - 1, N_HEAD, PART, DIM), BF16),
            pltpu.VMEM((2, PART, N_HEAD * DIM), BF16),
            pltpu.VMEM((8, DIM), jnp.int32),
            pltpu.SMEM((8, DIM), jnp.int32),
            pltpu.SemaphoreType.DMA((N_SEM,)),
            pltpu.SemaphoreType.DMA((N_SEM,)),
            pltpu.SemaphoreType.DMA((N_LOCAL,)),
        ],
        compiler_params=pltpu.CompilerParams(
            collective_id=0, has_side_effects=True, vmem_limit_bytes=56 * 1024 * 1024
        ),
        cost_estimate=pl.CostEstimate(flops=4_000_000_000, bytes_accessed=4_000_000, transcendentals=2_300_000),
        name="attention_core",
    )(queries, keys, values, grad_out.reshape(2, TOK // 2, COLS), owner_lists.T, doc_lengths)
    return finish(ao.reshape(TOK, COLS), gq, gk, gv)


def solution(mesh):
    placed = (
        P(("ctx", "head"), None),
        P(("ctx", "head"), None),
        P(("ctx", "head"), None),
        P("ctx", "head"),
        P(),
        P(),
    )
    return jax.shard_map(
        shards,
        mesh=mesh,
        in_specs=placed,
        out_specs=(
            P("ctx", "head"),
            P(("ctx", "head"), None),
            P(("ctx", "head"), None),
            P(("ctx", "head"), None),
        ),
        check_vma=False,
    )
```

```python
import functools
import math

import jax
import jax.numpy as jnp
from jax import lax
from jax.experimental import pallas as pl
from jax.experimental.pallas import tpu as pltpu
from jax.sharding import PartitionSpec as P

MESH = pl.DeviceIdType.MESH
BF16 = jnp.bfloat16
F32 = jnp.float32

N_CTX, N_HEAD = 32, 4
NZ, NY, NCORE = 4, 4, 2
PLANE = NY * NCORE
PLANES = 3
SLOTS = 9
PAIR = 256
TOK = 128
PART = 32
DIM = 128
GROUP = 8
ROWS = TOK * GROUP
COLS = GROUP * DIM
NDOCS = 16
MASKED = -1e30
SCALE = 1.0 / math.sqrt(DIM)
LOG2E = 1.0 / math.log(2.0)

XQ, G1, G2, A1, A2, DQ = range(6)
X0, X1, X2, Y1, YV, C1, CV, YP, XPV, XP, CP = (6, 8, 10, 12, 14, 16, 18, 20, 22, 24, 30)
N_SEM = 36
LK, LV, LRK, LRV, LQ, LG, LA, LDQ, LDK, LDV = range(10)
N_LOCAL = 10


def body(
    q_in, k_in, v_in, go_in, owned, doc_lengths,
    ao, gq, gk, gv,
    raw, kv, qs, gcol, gperm, gos, acol, aperm, out_rows, dq_rows,
    q_rows, q_cols, go_cols, probs, rounded_probs, parts, from_core, y_sum, from_y, sums, from_x, grads,
    slot_vec, slot_of, send, recv, local,
):
    c = lax.axis_index("ctx")
    h = lax.axis_index("head")
    z = c // PLANE
    idx = lax.rem(c, PLANE)
    y = idx // NCORE
    co = lax.rem(idx, NCORE)
    sib = c + 1 - 2 * co
    tile_row = pl.multiple_of(16 * (c // GROUP), 16)
    tile_head = lax.rem(c, GROUP)

    def ctx_at(zz, yy):
        return lax.rem(zz, NZ) * PLANE + lax.rem(yy, NY) * NCORE + co

    def push(src, dst, sem, ctx, head):
        copy = pltpu.make_async_remote_copy(
            src_ref=src, dst_ref=dst, send_sem=send.at[sem], recv_sem=recv.at[sem],
            device_id=(ctx, head), device_id_type=MESH,
        )
        copy.start()

    def drain(ref, sem):
        pltpu.make_async_copy(ref, ref, sem).wait()

    def cols(number, width):
        return pl.ds(pl.multiple_of(number * width, width), width)

    own_slot = NY + y

    local_copies = [
        pltpu.make_async_copy(k_in.at[:, cols(h, DIM)], kv.at[0, own_slot, co, cols(h, PART), :], local.at[LK]),
        pltpu.make_async_copy(v_in.at[:, cols(h, DIM)], kv.at[1, own_slot, co, cols(h, PART), :], local.at[LV]),
        pltpu.make_async_copy(k_in, raw.at[0], local.at[LRK]),
        pltpu.make_async_copy(v_in, raw.at[1], local.at[LRV]),
        pltpu.make_async_copy(q_in.at[:, cols(h, COLS)], qs.at[cols(h, PART), :], local.at[LQ]),
        pltpu.make_async_copy(
            go_in.at[:, pl.ds(tile_row, 16), cols(tile_head, DIM)], gcol.at[pl.ds(2 * c, 2)], local.at[LG]
        ),
    ]
    for copy in local_copies:
        copy.start()

    barrier = pltpu.get_barrier_semaphore()

    def greet(step, carry):
        pl.semaphore_signal(barrier, inc=1, device_id=(lax.rem(c + step, N_CTX), h), device_id_type=MESH)
        return carry

    lax.fori_loop(1, N_CTX, greet, 0)
    def greet_heads(ctx):
        for step in range(1, N_HEAD):
            pl.semaphore_signal(barrier, inc=1, device_id=(ctx, lax.rem(h + step, N_HEAD)), device_id_type=MESH)

    for ahead in range(NZ):
        greet_heads(ctx_at(z + ahead, y))

    lanes = lax.broadcasted_iota(jnp.int32, (8, DIM), 1)
    found = jnp.zeros((8, DIM), jnp.int32)
    for number in range(2 * N_CTX):
        found = jnp.where(lanes == owned[number % 2, number // 2], number, found)
    slot_vec[...] = found
    slot_copy = pltpu.make_async_copy(slot_vec, slot_of, local.at[LA])
    slot_copy.start()

    for copy in local_copies[:4]:
        copy.wait()
    slot_copy.wait()
    pl.semaphore_wait(barrier, N_CTX - 1 + NZ * (N_HEAD - 1))

    def tile_of(number):
        return pl.multiple_of(16 * (number // GROUP), 16), lax.rem(number, GROUP)

    def collect_grad(step, carry):
        to = lax.rem(c + step, N_CTX)
        row, head = tile_of(to)
        push(go_in.at[:, pl.ds(row, 16), cols(head, DIM)], gcol.at[pl.ds(2 * c, 2)], G1, to, h)
        return carry


    def by_head(which, slot, sem, ctx, first_step):
        for step in range(first_step, N_HEAD):
            to = lax.rem(h + step, N_HEAD)
            push(
                raw.at[which, :, cols(to, DIM)], kv.at[which, slot, co, cols(h, PART), :], sem + which, ctx, to
            )

    def first_hop(which):
        by_head(which, own_slot, X0, c, 1)
        by_head(which, y, X1, ctx_at(z + 1, y), 0)
        by_head(which, 2 * NY, X2, ctx_at(z + 2, y), 0)

    first_hop(0)
    first_hop(1)
    lax.fori_loop(1, N_CTX, collect_grad, 0)
    for step in range(1, N_HEAD):
        to = lax.rem(h + step, N_HEAD)
        push(q_in.at[:, cols(to, COLS)], qs.at[cols(h, PART), :], XQ, c, to)

    def along_y(which):
        drain(kv.at[0, 0, 0, pl.ds(0, 3 * PART), :], recv.at[X0 + which])
        for step in range(1, NY):
            yy = lax.rem(y + step, NY)

            @pl.when(yy > y)
            def _():
                push(kv.at[which, own_slot, co], kv.at[which, own_slot, co], YV + which, ctx_at(z, yy), h)

        drain(kv.at[0, 0, 0], recv.at[X1 + which])
        for step in range(1, NY):
            push(kv.at[which, y, co], kv.at[which, y, co], Y1 + which, ctx_at(z, y + step), h)
        drain(kv.at[0, 0, 0], recv.at[X2 + which])
        for step in range(1, NY):
            yy = lax.rem(y + step, NY)

            @pl.when(yy < y)
            def _():
                push(kv.at[which, 2 * NY, co], kv.at[which, own_slot, co], YV + which, ctx_at(z, yy), h)

    along_y(0)
    along_y(1)

    q_pos = c * TOK + lax.broadcasted_iota(jnp.int32, (1, TOK), 1)
    first = jnp.zeros((1, TOK), jnp.int32)
    begin = jnp.int32(0)
    for doc in range(NDOCS):
        first = jnp.where(q_pos >= begin, jnp.maximum(first, begin), first)
        begin = begin + doc_lengths[doc]

    local_copies[5].wait()
    drain(gcol.at[pl.ds(0, 62)], recv.at[G1])

    def arrange_grad(number, carry):
        gperm[number] = gcol[slot_of[0, number]]
        return carry

    lax.fori_loop(0, 2 * N_CTX, arrange_grad, 0, unroll=8)

    def deliver_grad(step, carry):
        to = lax.rem(c + step, N_CTX)
        push(
            gperm.at[pl.ds(2 * to, 2)], gos.at[tile_head, :, pl.ds(tile_row, 16), :], G2, to, h
        )
        return carry

    lax.fori_loop(1, N_CTX, deliver_grad, 0)
    gos[tile_head, :, pl.ds(tile_row, 16), :] = gperm[pl.ds(2 * c, 2)]

    local_copies[4].wait()
    drain(qs.at[pl.ds(0, 3 * PART), :], recv.at[XQ])
    for head in range(GROUP):
        rows = qs[:, head * DIM : (head + 1) * DIM]
        q_rows[head * TOK : (head + 1) * TOK, :] = rows
        q_cols[:, head * TOK : (head + 1) * TOK] = rows.T

    def to_other_core(which):
        drain(kv.at[0, pl.ds(0, 3), 0], recv.at[Y1 + which])
        push(kv.at[which, pl.ds(0, NY), co], kv.at[which, pl.ds(0, NY), co], C1 + which, sib, h)
        drain(kv.at[0, pl.ds(0, 3), 0], recv.at[YV + which])
        push(kv.at[which, pl.ds(NY, NY + 1), co], kv.at[which, pl.ds(NY, NY + 1), co], CV + which, sib, h)

    to_other_core(0)

    def position(slot):
        if slot < NY:
            return ((z - 1) * NY + slot) * PAIR
        if slot < 2 * NY:
            return (jnp.where(slot - NY <= y, z, z - 2) * NY + slot - NY) * PAIR
        return ((z - 2) * NY + y) * PAIR

    def scores(slot, peak):
        keys = kv[0, slot].reshape(PAIR, DIM)
        key_pos = position(slot) + lax.broadcasted_iota(jnp.int32, (PAIR, TOK), 0)
        bias = jnp.where((key_pos <= q_pos) & (key_pos >= first), 0.0, MASKED)
        bias = jnp.concatenate([bias] * GROUP, axis=1)
        block = jnp.dot(keys, q_cols[...], preferred_element_type=F32) * (SCALE * LOG2E) + bias
        probs[slot] = block
        return jnp.maximum(peak, jnp.max(block.reshape(PAIR // 8, 8, ROWS), axis=0))

    peak = jnp.full((8, ROWS), MASKED, F32)
    drain(kv.at[0, pl.ds(0, NY), 0], recv.at[C1])
    for slot in range(NY):
        peak = scores(slot, peak)
    drain(kv.at[0, pl.ds(0, NY + 1), 0], recv.at[CV])
    for slot in range(NY, SLOTS):
        peak = scores(slot, peak)
    peak = jnp.max(peak, axis=0, keepdims=True)
    to_other_core(1)

    total = jnp.zeros((8, ROWS), F32)
    for slot in range(SLOTS):
        block = jnp.exp2(probs[slot] - peak)
        probs[slot] = block
        rounded_probs[slot] = block.astype(BF16)
        total = total + jnp.sum(block.reshape(PAIR // 8, 8, ROWS), axis=0)
    drain(kv.at[0, pl.ds(0, NY), 0], recv.at[C1 + 1])
    drain(kv.at[0, pl.ds(0, NY + 1), 0], recv.at[CV + 1])
    accum = jnp.zeros((DIM, ROWS), F32)
    for slot in range(SLOTS):
        values = kv[1, slot].reshape(PAIR, DIM)
        accum = accum + jnp.dot(values.T, rounded_probs[slot], preferred_element_type=F32)
    inverse = 1.0 / jnp.sum(total, axis=0, keepdims=True)
    rounded = (accum * inverse).astype(BF16)
    for head in range(GROUP):
        rows = rounded[:, head * TOK : (head + 1) * TOK].T
        out_rows[head, 0] = rows[:64]
        out_rows[head, 1] = rows[64:]

    def collect_out(step, carry):
        to = lax.rem(c + step, N_CTX)
        row, head = tile_of(to)
        push(out_rows.at[head, :, pl.ds(row, 16), :], acol.at[pl.ds(2 * c, 2)], A1, to, h)
        return carry

    lax.fori_loop(1, N_CTX, collect_out, 0)
    acol[pl.ds(2 * c, 2)] = out_rows[tile_head, :, pl.ds(tile_row, 16), :]

    drain(gperm.at[pl.ds(0, 62)], recv.at[G2])
    for head in range(GROUP):
        go_cols[:, head * TOK : (head + 1) * TOK] = gos[head].reshape(TOK, DIM).T
    delta = jnp.sum(go_cols[...].astype(F32) * rounded.astype(F32), axis=0, keepdims=True)

    beside = [lax.rem(y + step, NY) for step in range(1, NY)]
    virtual = [NY + yy for yy in beside]
    rest = [y, 2 * NY, own_slot]

    def both_cores(which, slot):
        return parts[which, slot, co].astype(F32) + from_core[which, slot].astype(F32)

    def home(which, number, sem, ctx, first_step):
        for step in range(first_step, N_HEAD):
            to = lax.rem(h + step, N_HEAD)
            push(sums.at[which, number, cols(to, PART), :], from_x.at[which, number, h], sem, ctx, to)

    def beside_home(which):
        for step, slot in enumerate(beside):
            y_sum[which, step] = both_cores(which, slot).astype(BF16)
            push(y_sum.at[which, step], from_y.at[which, step], YP + which, ctx_at(z, y + step + 1), h)

    def virtual_home(which):
        for step, slot in enumerate(virtual):
            sums[which, PLANES + step] = both_cores(which, slot).astype(BF16)
            plane = jnp.where(beside[step] <= y, z, z + 2)
            home(which, PLANES + step, XPV + which, ctx_at(plane, beside[step]), 0)

    def rest_home(which):
        sums[which, 0] = both_cores(which, 2 * NY).astype(BF16)
        home(which, 0, XP + 3 * which, ctx_at(z + 2, y), 0)
        sums[which, 2] = both_cores(which, own_slot).astype(BF16)
        home(which, 2, XP + 3 * which + 2, c, 1)
        from_x[which, 2, h] = sums[which, 2, cols(h, PART), :]

    def before_home(which):
        drain(from_y.at[0], recv.at[YP + which])
        before = both_cores(which, y)
        for step in range(NY - 1):
            before = before + from_y[which, step].astype(F32)
        sums[which, 1] = before.astype(BF16)
        home(which, 1, XP + 3 * which + 1, ctx_at(z + 3, y), 0)

    def value_group(slots, sem):
        for slot in slots:
            weights = (probs[slot] * inverse).astype(BF16)
            part = jnp.dot(weights, gos[...].reshape(ROWS, DIM), preferred_element_type=F32)
            parts[1, slot] = part.astype(BF16).reshape(NCORE, TOK, DIM)
        for slot in slots:
            push(parts.at[1, slot, 1 - co], from_core.at[1, slot], sem, sib, h)

    def key_group(slots, sem, query_grad):
        for slot in slots:
            keys, values = kv[0, slot].reshape(PAIR, DIM), kv[1, slot].reshape(PAIR, DIM)
            pushed = jnp.dot(values, go_cols[...], preferred_element_type=F32)
            slopes = (probs[slot] * inverse * (pushed - delta)).astype(BF16)
            part = jnp.dot(slopes, q_rows[...], preferred_element_type=F32) * SCALE
            parts[0, slot] = part.astype(BF16).reshape(NCORE, TOK, DIM)
            query_grad = query_grad + jnp.dot(keys.T, slopes, preferred_element_type=F32)
        for slot in slots:
            push(parts.at[0, slot, 1 - co], from_core.at[0, slot], sem, sib, h)
        return query_grad

    def drain_core(sem):
        drain(from_core.at[0, pl.ds(0, 3)], recv.at[sem])

    value_group(beside, CP)
    value_group(virtual, CP + 1)
    value_group(rest, CP + 2)
    query_grad = jnp.zeros((DIM, ROWS), F32)
    query_grad = key_group(beside, CP + 3, query_grad)
    drain_core(CP)
    beside_home(1)
    drain_core(CP + 1)
    virtual_home(1)
    drain_core(CP + 2)
    rest_home(1)
    query_grad = key_group(virtual, CP + 4, query_grad)
    drain_core(CP + 3)
    beside_home(0)
    query_grad = key_group(rest, CP + 5, query_grad)
    drain_core(CP + 4)
    virtual_home(0)

    query_grad = (query_grad * SCALE).astype(BF16)
    for head in range(GROUP):
        dq_rows[:, head * DIM : (head + 1) * DIM] = query_grad[:, head * TOK : (head + 1) * TOK].T
    for step in range(1, N_HEAD):
        to = lax.rem(h + step, N_HEAD)
        push(dq_rows.at[cols(to, PART), :], gq.at[:, cols(h, COLS)], DQ, c, to)
    own_dq = pltpu.make_async_copy(dq_rows.at[cols(h, PART), :], gq.at[:, cols(h, COLS)], local.at[LDQ])
    own_dq.start()

    drain(acol.at[pl.ds(0, 62)], recv.at[A1])

    def arrange_out(number, carry):
        aperm[2 * number] = acol[owned[0, number]]
        aperm[2 * number + 1] = acol[owned[1, number]]
        return carry

    lax.fori_loop(0, N_CTX, arrange_out, 0, unroll=4)

    def deliver_out(step, carry):
        to = lax.rem(c + step, N_CTX)
        push(
            aperm.at[pl.ds(2 * to, 2)], ao.at[:, pl.ds(tile_row, 16), cols(tile_head, DIM)], A2, to, h
        )
        return carry

    lax.fori_loop(1, N_CTX, deliver_out, 0)
    own_out = pltpu.make_async_copy(
        aperm.at[pl.ds(2 * c, 2)], ao.at[:, pl.ds(tile_row, 16), cols(tile_head, DIM)], local.at[LA]
    )
    own_out.start()
    drain_core(CP + 5)
    rest_home(0)
    before_home(1)
    before_home(0)

    for which in (1, 0):
        drain(from_x.at[0, pl.ds(PLANES, 3)], recv.at[XPV + which])
        drain(from_x.at[0, 0], recv.at[XP + 3 * which])
        drain(from_x.at[0, 0, pl.ds(0, 3)], recv.at[XP + 3 * which + 2])
        drain(from_x.at[0, 0], recv.at[XP + 3 * which + 1])
        for head in range(N_HEAD):
            piece = from_x[which, 0, head].astype(F32)
            for number in range(1, PLANES + NY - 1):
                piece = piece + from_x[which, number, head].astype(F32)
            grads[which, :, head * DIM : (head + 1) * DIM] = piece.astype(BF16)
    own_dk = pltpu.make_async_copy(grads.at[0], gk, local.at[LDK])
    own_dv = pltpu.make_async_copy(grads.at[1], gv, local.at[LDV])
    own_dk.start()
    own_dv.start()

    three_cols = pl.ds(0, 3 * COLS)
    drain(gperm.at[pl.ds(0, 62)], recv.at[A2])
    drain(gq.at[:, three_cols], recv.at[DQ])
    for copy in (own_out, own_dq, own_dk, own_dv):
        copy.wait()
    for sem in (G1, G2, A1, A2):
        drain(gperm.at[pl.ds(0, 62)], send.at[sem])
    for sem in (XQ, DQ):
        drain(gq.at[:, three_cols], send.at[sem])
    for which in range(2):
        for sem in (X0 + which, XP + 3 * which + 2):
            drain(from_x.at[0, 0, pl.ds(0, 3)], send.at[sem])
        for sem in (X1 + which, X2 + which, XP + 3 * which, XP + 3 * which + 1):
            drain(from_x.at[0, 0], send.at[sem])
        for sem in (Y1, YV, YP, XPV):
            drain(from_y.at[0], send.at[sem + which])
        for sem in range(3):
            drain(from_y.at[0], send.at[CP + 3 * which + sem])
        drain(kv.at[0, pl.ds(0, NY), 0], send.at[C1 + which])
        drain(kv.at[0, pl.ds(0, NY + 1), 0], send.at[CV + which])


def finish_body(ao, gq, gk, gv, ao_out, gq_out, gk_out, gv_out, sems):
    copies = [
        pltpu.make_async_copy(src, dst, sems.at[number])
        for number, (src, dst) in enumerate(((ao, ao_out), (gq, gq_out), (gk, gk_out), (gv, gv_out)))
    ]
    for copy in copies:
        copy.start()
    for copy in copies:
        copy.wait()


def finish(*arrays):
    anywhere = pl.BlockSpec(memory_space=pltpu.VMEM)
    hbm = pl.BlockSpec(memory_space=pltpu.HBM)
    return pl.pallas_call(
        finish_body,
        out_shape=tuple(jax.ShapeDtypeStruct(array.shape, array.dtype) for array in arrays),
        in_specs=[anywhere] * 4,
        out_specs=(hbm,) * 4,
        scratch_shapes=[pltpu.SemaphoreType.DMA((4,))],
        name="write_outputs",
    )(*arrays)


def shards(queries, keys, values, grad_out, owner_lists, doc_lengths):
    hbm = pl.BlockSpec(memory_space=pltpu.HBM)
    smem = pl.BlockSpec(memory_space=pltpu.SMEM)
    block = (TOK, DIM)
    ao, gq, gk, gv = pl.pallas_call(
        body,
        out_shape=(
            jax.ShapeDtypeStruct((2, TOK // 2, COLS), BF16),
            jax.ShapeDtypeStruct((PART, N_HEAD * COLS), BF16),
            jax.ShapeDtypeStruct((PART, N_HEAD * DIM), BF16),
            jax.ShapeDtypeStruct((PART, N_HEAD * DIM), BF16),
        ),
        in_specs=[hbm] * 4 + [smem] * 2,
        out_specs=(hbm,) * 4,
        scratch_shapes=[
            pltpu.VMEM((2, PART, N_HEAD * DIM), BF16),
            pltpu.VMEM((2, SLOTS, NCORE) + block, BF16),
            pltpu.VMEM((TOK, COLS), BF16),
            pltpu.VMEM((2 * N_CTX, 16, DIM), BF16),
            pltpu.VMEM((2 * N_CTX, 16, DIM), BF16),
            pltpu.VMEM((GROUP, 2, TOK // 2, DIM), BF16),
            pltpu.VMEM((2 * N_CTX, 16, DIM), BF16),
            pltpu.VMEM((2 * N_CTX, 16, DIM), BF16),
            pltpu.VMEM((GROUP, 2, TOK // 2, DIM), BF16),
            pltpu.VMEM((TOK, COLS), BF16),
            pltpu.VMEM((ROWS, DIM), BF16),
            pltpu.VMEM((DIM, ROWS), BF16),
            pltpu.VMEM((DIM, ROWS), BF16),
            pltpu.VMEM((SLOTS, PAIR, ROWS), F32),
            pltpu.VMEM((SLOTS, PAIR, ROWS), BF16),
            pltpu.VMEM((2, SLOTS, NCORE) + block, BF16),
            pltpu.VMEM((2, SLOTS) + block, BF16),
            pltpu.VMEM((2, NY - 1) + block, BF16),
            pltpu.VMEM((2, NY - 1) + block, BF16),
            pltpu.VMEM((2, PLANES + NY - 1) + block, BF16),
            pltpu.VMEM((2, PLANES + NY - 1, N_HEAD, PART, DIM), BF16),
            pltpu.VMEM((2, PART, N_HEAD * DIM), BF16),
            pltpu.VMEM((8, DIM), jnp.int32),
            pltpu.SMEM((8, DIM), jnp.int32),
            pltpu.SemaphoreType.DMA((N_SEM,)),
            pltpu.SemaphoreType.DMA((N_SEM,)),
            pltpu.SemaphoreType.DMA((N_LOCAL,)),
        ],
        compiler_params=pltpu.CompilerParams(
            collective_id=0, has_side_effects=True, vmem_limit_bytes=56 * 1024 * 1024
        ),
        cost_estimate=pl.CostEstimate(flops=4_000_000_000, bytes_accessed=4_000_000, transcendentals=2_300_000),
        name="attention_core",
    )(queries, keys, values, grad_out.reshape(2, TOK // 2, COLS), owner_lists.T, doc_lengths)
    return finish(ao.reshape(TOK, COLS), gq, gk, gv)


def solution(mesh):
    placed = (
        P(("ctx", "head"), None),
        P(("ctx", "head"), None),
        P(("ctx", "head"), None),
        P("ctx", "head"),
        P(),
        P(),
    )
    return jax.shard_map(
        shards,
        mesh=mesh,
        in_specs=placed,
        out_specs=(
            P("ctx", "head"),
            P(("ctx", "head"), None),
            P(("ctx", "head"), None),
            P(("ctx", "head"), None),
        ),
        check_vma=False,
    )
```

```python
import functools
import math

import jax
import jax.numpy as jnp
from jax import lax
from jax.experimental import pallas as pl
from jax.experimental.pallas import tpu as pltpu
from jax.sharding import PartitionSpec as P

MESH = pl.DeviceIdType.MESH
BF16 = jnp.bfloat16
F32 = jnp.float32

N_CTX, N_HEAD = 32, 4
NZ, NY, NCORE = 4, 4, 2
PLANE = NY * NCORE
PLANES = 3
SLOTS = 9
PAIR = 256
TOK = 128
PART = 32
DIM = 128
GROUP = 8
ROWS = TOK * GROUP
COLS = GROUP * DIM
NDOCS = 16
MASKED = -1e30
SCALE = 1.0 / math.sqrt(DIM)
LOG2E = 1.0 / math.log(2.0)

XQ, G1, G2, A1, A2, DQ = range(6)
X0, X1, X2, Y1, YV, C1, CV, YP, XPV, XP, CP = (6, 8, 10, 12, 14, 16, 18, 20, 22, 24, 30)
N_SEM = 36
LK, LV, LQ, LG, LS, LA = range(6)
N_LOCAL = 6


def body(
    q_in, k_in, v_in, go_in, owned, doc_lengths,
    ao, gq, gk, gv,
    kv, qs, gcol, gperm, gos, acol, aperm, out_rows, dq_rows,
    q_rows, q_cols, go_cols, probs, rounded_probs, parts, from_core, y_sum, from_y, sums, from_x,
    slot_vec, slot_of, send, recv, local,
):
    c = lax.axis_index("ctx")
    h = lax.axis_index("head")
    z = c // PLANE
    idx = lax.rem(c, PLANE)
    y = idx // NCORE
    co = lax.rem(idx, NCORE)
    sib = c + 1 - 2 * co
    tile_row = pl.multiple_of(16 * (c // GROUP), 16)
    tile_head = lax.rem(c, GROUP)

    def ctx_at(zz, yy):
        return lax.rem(zz, NZ) * PLANE + lax.rem(yy, NY) * NCORE + co

    def push(src, dst, sem, ctx, head):
        copy = pltpu.make_async_remote_copy(
            src_ref=src, dst_ref=dst, send_sem=send.at[sem], recv_sem=recv.at[sem],
            device_id=(ctx, head), device_id_type=MESH,
        )
        copy.start()

    def drain(ref, sem):
        pltpu.make_async_copy(ref, ref, sem).wait()

    def cols(number, width):
        return pl.ds(pl.multiple_of(number * width, width), width)

    own_slot = NY + y

    local_copies = [
        pltpu.make_async_copy(k_in.at[:, cols(h, DIM)], kv.at[0, own_slot, co, cols(h, PART), :], local.at[LK]),
        pltpu.make_async_copy(v_in.at[:, cols(h, DIM)], kv.at[1, own_slot, co, cols(h, PART), :], local.at[LV]),
        pltpu.make_async_copy(q_in.at[:, cols(h, COLS)], qs.at[cols(h, PART), :], local.at[LQ]),
        pltpu.make_async_copy(
            go_in.at[:, pl.ds(tile_row, 16), cols(tile_head, DIM)], gcol.at[pl.ds(2 * c, 2)], local.at[LG]
        ),
    ]
    for copy in local_copies:
        copy.start()

    barrier = pltpu.get_barrier_semaphore()

    def greet(step, carry):
        pl.semaphore_signal(barrier, inc=1, device_id=(lax.rem(c + step, N_CTX), h), device_id_type=MESH)
        return carry

    lax.fori_loop(1, N_CTX, greet, 0)
    def greet_heads(ctx):
        for step in range(1, N_HEAD):
            pl.semaphore_signal(barrier, inc=1, device_id=(ctx, lax.rem(h + step, N_HEAD)), device_id_type=MESH)

    for ahead in range(NZ):
        greet_heads(ctx_at(z + ahead, y))

    pl.semaphore_wait(barrier, N_CTX - 1 + NZ * (N_HEAD - 1))

    def tile_of(number):
        return pl.multiple_of(16 * (number // GROUP), 16), lax.rem(number, GROUP)

    def collect_grad(step, carry):
        to = lax.rem(c + step, N_CTX)
        row, head = tile_of(to)
        push(go_in.at[:, pl.ds(row, 16), cols(head, DIM)], gcol.at[pl.ds(2 * c, 2)], G1, to, h)
        return carry


    def by_head(which, slot, sem, ctx, first_step):
        for step in range(first_step, N_HEAD):
            to = lax.rem(h + step, N_HEAD)
            push(
                (k_in, v_in)[which].at[:, cols(to, DIM)], kv.at[which, slot, co, cols(h, PART), :], sem + which, ctx, to
            )

    def first_hop(which):
        by_head(which, own_slot, X0, c, 1)
        by_head(which, y, X1, ctx_at(z + 1, y), 0)
        by_head(which, 2 * NY, X2, ctx_at(z + 2, y), 0)

    first_hop(0)
    first_hop(1)
    lax.fori_loop(1, N_CTX, collect_grad, 0)
    for step in range(1, N_HEAD):
        to = lax.rem(h + step, N_HEAD)
        push(q_in.at[:, cols(to, COLS)], qs.at[cols(h, PART), :], XQ, c, to)

    def along_y(which):
        drain(kv.at[0, 0, 0, pl.ds(0, 3 * PART), :], recv.at[X0 + which])
        for step in range(1, NY):
            yy = lax.rem(y + step, NY)

            @pl.when(yy > y)
            def _():
                push(kv.at[which, own_slot, co], kv.at[which, own_slot, co], YV + which, ctx_at(z, yy), h)

        drain(kv.at[0, 0, 0], recv.at[X1 + which])
        for step in range(1, NY):
            push(kv.at[which, y, co], kv.at[which, y, co], Y1 + which, ctx_at(z, y + step), h)
        drain(kv.at[0, 0, 0], recv.at[X2 + which])
        for step in range(1, NY):
            yy = lax.rem(y + step, NY)

            @pl.when(yy < y)
            def _():
                push(kv.at[which, 2 * NY, co], kv.at[which, own_slot, co], YV + which, ctx_at(z, yy), h)

    lanes = lax.broadcasted_iota(jnp.int32, (8, DIM), 1)
    found = jnp.zeros((8, DIM), jnp.int32)
    for number in range(2 * N_CTX):
        found = jnp.where(lanes == owned[number % 2, number // 2], number, found)
    slot_vec[...] = found
    slot_copy = pltpu.make_async_copy(slot_vec, slot_of, local.at[LS])
    slot_copy.start()

    local_copies[0].wait()
    along_y(0)
    local_copies[1].wait()
    along_y(1)

    q_pos = c * TOK + lax.broadcasted_iota(jnp.int32, (1, TOK), 1)
    first = jnp.zeros((1, TOK), jnp.int32)
    begin = jnp.int32(0)
    for doc in range(NDOCS):
        first = jnp.where(q_pos >= begin, jnp.maximum(first, begin), first)
        begin = begin + doc_lengths[doc]

    local_copies[3].wait()
    slot_copy.wait()
    drain(gcol.at[pl.ds(0, 62)], recv.at[G1])

    def arrange_grad(number, carry):
        gperm[number] = gcol[slot_of[0, number]]
        return carry

    lax.fori_loop(0, 2 * N_CTX, arrange_grad, 0, unroll=8)

    def deliver_grad(step, carry):
        to = lax.rem(c + step, N_CTX)
        push(
            gperm.at[pl.ds(2 * to, 2)], gos.at[tile_head, :, pl.ds(tile_row, 16), :], G2, to, h
        )
        return carry

    lax.fori_loop(1, N_CTX, deliver_grad, 0)
    gos[tile_head, :, pl.ds(tile_row, 16), :] = gperm[pl.ds(2 * c, 2)]

    local_copies[2].wait()
    drain(qs.at[pl.ds(0, 3 * PART), :], recv.at[XQ])
    for head in range(GROUP):
        rows = qs[:, head * DIM : (head + 1) * DIM]
        q_rows[head * TOK : (head + 1) * TOK, :] = rows
        q_cols[:, head * TOK : (head + 1) * TOK] = rows.T

    def to_other_core(which):
        drain(kv.at[0, pl.ds(0, 3), 0], recv.at[Y1 + which])
        push(kv.at[which, pl.ds(0, NY), co], kv.at[which, pl.ds(0, NY), co], C1 + which, sib, h)
        drain(kv.at[0, pl.ds(0, 3), 0], recv.at[YV + which])
        push(kv.at[which, pl.ds(NY, NY + 1), co], kv.at[which, pl.ds(NY, NY + 1), co], CV + which, sib, h)

    to_other_core(0)

    def position(slot):
        if slot < NY:
            return ((z - 1) * NY + slot) * PAIR
        if slot < 2 * NY:
            return (jnp.where(slot - NY <= y, z, z - 2) * NY + slot - NY) * PAIR
        return ((z - 2) * NY + y) * PAIR

    def scores(slot, peak):
        keys = kv[0, slot].reshape(PAIR, DIM)
        key_pos = position(slot) + lax.broadcasted_iota(jnp.int32, (PAIR, TOK), 0)
        bias = jnp.where((key_pos <= q_pos) & (key_pos >= first), 0.0, MASKED)
        bias = jnp.concatenate([bias] * GROUP, axis=1)
        block = jnp.dot(keys, q_cols[...], preferred_element_type=F32) * (SCALE * LOG2E) + bias
        probs[slot] = block
        return jnp.maximum(peak, jnp.max(block.reshape(PAIR // 8, 8, ROWS), axis=0))

    peak = jnp.full((8, ROWS), MASKED, F32)
    drain(kv.at[0, pl.ds(0, NY), 0], recv.at[C1])
    for slot in range(NY):
        peak = scores(slot, peak)
    drain(kv.at[0, pl.ds(0, NY + 1), 0], recv.at[CV])
    for slot in range(NY, SLOTS):
        peak = scores(slot, peak)
    peak = jnp.max(peak, axis=0, keepdims=True)
    to_other_core(1)

    total = jnp.zeros((8, ROWS), F32)
    for slot in range(SLOTS):
        block = jnp.exp2(probs[slot] - peak)
        probs[slot] = block
        rounded_probs[slot] = block.astype(BF16)
        total = total + jnp.sum(block.reshape(PAIR // 8, 8, ROWS), axis=0)
    drain(kv.at[0, pl.ds(0, NY), 0], recv.at[C1 + 1])
    drain(kv.at[0, pl.ds(0, NY + 1), 0], recv.at[CV + 1])
    accum = jnp.zeros((DIM, ROWS), F32)
    for slot in range(SLOTS):
        values = kv[1, slot].reshape(PAIR, DIM)
        accum = accum + jnp.dot(values.T, rounded_probs[slot], preferred_element_type=F32)
    inverse = 1.0 / jnp.sum(total, axis=0, keepdims=True)
    rounded = (accum * inverse).astype(BF16)
    for head in range(GROUP):
        rows = rounded[:, head * TOK : (head + 1) * TOK].T
        out_rows[head, 0] = rows[:64]
        out_rows[head, 1] = rows[64:]

    def collect_out(step, carry):
        to = lax.rem(c + step, N_CTX)
        row, head = tile_of(to)
        push(out_rows.at[head, :, pl.ds(row, 16), :], acol.at[pl.ds(2 * c, 2)], A1, to, h)
        return carry

    lax.fori_loop(1, N_CTX, collect_out, 0)
    acol[pl.ds(2 * c, 2)] = out_rows[tile_head, :, pl.ds(tile_row, 16), :]

    drain(gperm.at[pl.ds(0, 62)], recv.at[G2])
    for head in range(GROUP):
        go_cols[:, head * TOK : (head + 1) * TOK] = gos[head].reshape(TOK, DIM).T
    delta = jnp.sum(go_cols[...].astype(F32) * rounded.astype(F32), axis=0, keepdims=True)

    beside = [lax.rem(y + step, NY) for step in range(1, NY)]
    virtual = [NY + yy for yy in beside]
    rest = [y, 2 * NY, own_slot]

    def both_cores(which, slot):
        return parts[which, slot, co].astype(F32) + from_core[which, slot].astype(F32)

    def home(which, number, sem, ctx, first_step):
        for step in range(first_step, N_HEAD):
            to = lax.rem(h + step, N_HEAD)
            push(sums.at[which, number, cols(to, PART), :], from_x.at[which, number, h], sem, ctx, to)

    def beside_home(which):
        for step, slot in enumerate(beside):
            y_sum[which, step] = both_cores(which, slot).astype(BF16)
            push(y_sum.at[which, step], from_y.at[which, step], YP + which, ctx_at(z, y + step + 1), h)

    def virtual_home(which):
        for step, slot in enumerate(virtual):
            sums[which, PLANES + step] = both_cores(which, slot).astype(BF16)
            plane = jnp.where(beside[step] <= y, z, z + 2)
            home(which, PLANES + step, XPV + which, ctx_at(plane, beside[step]), 0)

    def rest_home(which):
        sums[which, 0] = both_cores(which, 2 * NY).astype(BF16)
        home(which, 0, XP + 3 * which, ctx_at(z + 2, y), 0)
        sums[which, 2] = both_cores(which, own_slot).astype(BF16)
        home(which, 2, XP + 3 * which + 2, c, 1)
        from_x[which, 2, h] = sums[which, 2, cols(h, PART), :]

    def before_home(which):
        drain(from_y.at[0], recv.at[YP + which])
        before = both_cores(which, y)
        for step in range(NY - 1):
            before = before + from_y[which, step].astype(F32)
        sums[which, 1] = before.astype(BF16)
        home(which, 1, XP + 3 * which + 1, ctx_at(z + 3, y), 0)

    def value_group(slots, sem):
        for slot in slots:
            weights = (probs[slot] * inverse).astype(BF16)
            part = jnp.dot(weights, gos[...].reshape(ROWS, DIM), preferred_element_type=F32)
            parts[1, slot] = part.astype(BF16).reshape(NCORE, TOK, DIM)
        for slot in slots:
            push(parts.at[1, slot, 1 - co], from_core.at[1, slot], sem, sib, h)

    def key_group(slots, sem, query_grad):
        for slot in slots:
            keys, values = kv[0, slot].reshape(PAIR, DIM), kv[1, slot].reshape(PAIR, DIM)
            pushed = jnp.dot(values, go_cols[...], preferred_element_type=F32)
            slopes = (probs[slot] * inverse * (pushed - delta)).astype(BF16)
            part = jnp.dot(slopes, q_rows[...], preferred_element_type=F32) * SCALE
            parts[0, slot] = part.astype(BF16).reshape(NCORE, TOK, DIM)
            query_grad = query_grad + jnp.dot(keys.T, slopes, preferred_element_type=F32)
        for slot in slots:
            push(parts.at[0, slot, 1 - co], from_core.at[0, slot], sem, sib, h)
        return query_grad

    def drain_core(sem):
        drain(from_core.at[0, pl.ds(0, 3)], recv.at[sem])

    value_group(beside, CP)
    value_group(virtual, CP + 1)
    value_group(rest, CP + 2)
    query_grad = jnp.zeros((DIM, ROWS), F32)
    query_grad = key_group(beside, CP + 3, query_grad)
    drain_core(CP)
    beside_home(1)
    drain_core(CP + 1)
    virtual_home(1)
    drain_core(CP + 2)
    rest_home(1)
    query_grad = key_group(virtual, CP + 4, query_grad)
    drain_core(CP + 3)
    beside_home(0)
    query_grad = key_group(rest, CP + 5, query_grad)
    drain_core(CP + 4)
    virtual_home(0)

    query_grad = (query_grad * SCALE).astype(BF16)
    for head in range(GROUP):
        dq_rows[:, head * DIM : (head + 1) * DIM] = query_grad[:, head * TOK : (head + 1) * TOK].T
    for step in range(1, N_HEAD):
        to = lax.rem(h + step, N_HEAD)
        push(dq_rows.at[cols(to, PART), :], gq.at[:, cols(h, COLS)], DQ, c, to)
    gq[:, cols(h, COLS)] = dq_rows[cols(h, PART), :]

    drain(acol.at[pl.ds(0, 62)], recv.at[A1])

    def arrange_out(number, carry):
        aperm[2 * number] = acol[owned[0, number]]
        aperm[2 * number + 1] = acol[owned[1, number]]
        return carry

    lax.fori_loop(0, N_CTX, arrange_out, 0, unroll=4)

    def deliver_out(step, carry):
        to = lax.rem(c + step, N_CTX)
        push(
            aperm.at[pl.ds(2 * to, 2)], ao.at[:, pl.ds(tile_row, 16), cols(tile_head, DIM)], A2, to, h
        )
        return carry

    lax.fori_loop(1, N_CTX, deliver_out, 0)
    own_out = pltpu.make_async_copy(
        aperm.at[pl.ds(2 * c, 2)], ao.at[:, pl.ds(tile_row, 16), cols(tile_head, DIM)], local.at[LA]
    )
    own_out.start()
    drain_core(CP + 5)
    rest_home(0)
    before_home(1)
    before_home(0)

    for which in (1, 0):
        drain(from_x.at[0, pl.ds(PLANES, 3)], recv.at[XPV + which])
        drain(from_x.at[0, 0], recv.at[XP + 3 * which])
        drain(from_x.at[0, 0, pl.ds(0, 3)], recv.at[XP + 3 * which + 2])
        drain(from_x.at[0, 0], recv.at[XP + 3 * which + 1])
        for head in range(N_HEAD):
            piece = from_x[which, 0, head].astype(F32)
            for number in range(1, PLANES + NY - 1):
                piece = piece + from_x[which, number, head].astype(F32)
            (gk, gv)[which][:, head * DIM : (head + 1) * DIM] = piece.astype(BF16)
    three_cols = pl.ds(0, 3 * COLS)
    drain(gperm.at[pl.ds(0, 62)], recv.at[A2])
    drain(gq.at[:, three_cols], recv.at[DQ])
    own_out.wait()
    for sem in (G1, G2, A1, A2):
        drain(gperm.at[pl.ds(0, 62)], send.at[sem])
    for sem in (XQ, DQ):
        drain(gq.at[:, three_cols], send.at[sem])
    for which in range(2):
        for sem in (X0 + which, XP + 3 * which + 2):
            drain(from_x.at[0, 0, pl.ds(0, 3)], send.at[sem])
        for sem in (X1 + which, X2 + which, XP + 3 * which, XP + 3 * which + 1):
            drain(from_x.at[0, 0], send.at[sem])
        for sem in (Y1, YV, YP, XPV):
            drain(from_y.at[0], send.at[sem + which])
        for sem in range(3):
            drain(from_y.at[0], send.at[CP + 3 * which + sem])
        drain(kv.at[0, pl.ds(0, NY), 0], send.at[C1 + which])
        drain(kv.at[0, pl.ds(0, NY + 1), 0], send.at[CV + which])


def finish_body(ao, gq, gk, gv, ao_out, gq_out, gk_out, gv_out, sems):
    copies = [
        pltpu.make_async_copy(src, dst, sems.at[number])
        for number, (src, dst) in enumerate(((ao, ao_out), (gq, gq_out), (gk, gk_out), (gv, gv_out)))
    ]
    for copy in copies:
        copy.start()
    for copy in copies:
        copy.wait()


def finish(*arrays):
    anywhere = pl.BlockSpec(memory_space=pltpu.VMEM)
    arrays = [pltpu.with_memory_space_constraint(array, pltpu.VMEM) for array in arrays]
    hbm = pl.BlockSpec(memory_space=pltpu.HBM)
    return pl.pallas_call(
        finish_body,
        out_shape=tuple(jax.ShapeDtypeStruct(array.shape, array.dtype) for array in arrays),
        in_specs=[anywhere] * 4,
        out_specs=(hbm,) * 4,
        scratch_shapes=[pltpu.SemaphoreType.DMA((4,))],
        name="write_outputs",
    )(*arrays)


def shards(queries, keys, values, grad_out, owner_lists, doc_lengths):
    hbm = pl.BlockSpec(memory_space=pltpu.HBM)
    smem = pl.BlockSpec(memory_space=pltpu.SMEM)
    block = (TOK, DIM)
    ao, gq, gk, gv = pl.pallas_call(
        body,
        out_shape=(
            pltpu.VMEM((2, TOK // 2, COLS), BF16),
            pltpu.VMEM((PART, N_HEAD * COLS), BF16),
            pltpu.VMEM((PART, N_HEAD * DIM), BF16),
            pltpu.VMEM((PART, N_HEAD * DIM), BF16),
        ),
        in_specs=[hbm] * 4 + [smem] * 2,
        out_specs=(pl.BlockSpec(memory_space=pltpu.VMEM),) * 4,
        scratch_shapes=[
            pltpu.VMEM((2, SLOTS, NCORE) + block, BF16),
            pltpu.VMEM((TOK, COLS), BF16),
            pltpu.VMEM((2 * N_CTX, 16, DIM), BF16),
            pltpu.VMEM((2 * N_CTX, 16, DIM), BF16),
            pltpu.VMEM((GROUP, 2, TOK // 2, DIM), BF16),
            pltpu.VMEM((2 * N_CTX, 16, DIM), BF16),
            pltpu.VMEM((2 * N_CTX, 16, DIM), BF16),
            pltpu.VMEM((GROUP, 2, TOK // 2, DIM), BF16),
            pltpu.VMEM((TOK, COLS), BF16),
            pltpu.VMEM((ROWS, DIM), BF16),
            pltpu.VMEM((DIM, ROWS), BF16),
            pltpu.VMEM((DIM, ROWS), BF16),
            pltpu.VMEM((SLOTS, PAIR, ROWS), F32),
            pltpu.VMEM((SLOTS, PAIR, ROWS), BF16),
            pltpu.VMEM((2, SLOTS, NCORE) + block, BF16),
            pltpu.VMEM((2, SLOTS) + block, BF16),
            pltpu.VMEM((2, NY - 1) + block, BF16),
            pltpu.VMEM((2, NY - 1) + block, BF16),
            pltpu.VMEM((2, PLANES + NY - 1) + block, BF16),
            pltpu.VMEM((2, PLANES + NY - 1, N_HEAD, PART, DIM), BF16),
            pltpu.VMEM((8, DIM), jnp.int32),
            pltpu.SMEM((8, DIM), jnp.int32),
            pltpu.SemaphoreType.DMA((N_SEM,)),
            pltpu.SemaphoreType.DMA((N_SEM,)),
            pltpu.SemaphoreType.DMA((N_LOCAL,)),
        ],
        compiler_params=pltpu.CompilerParams(
            collective_id=0, has_side_effects=True, vmem_limit_bytes=56 * 1024 * 1024
        ),
        cost_estimate=pl.CostEstimate(flops=4_000_000_000, bytes_accessed=4_000_000, transcendentals=2_300_000),
        name="attention_core",
    )(queries, keys, values, grad_out.reshape(2, TOK // 2, COLS), owner_lists.T, doc_lengths)
    return finish(ao.reshape(TOK, COLS), gq, gk, gv)


def solution(mesh):
    placed = (
        P(("ctx", "head"), None),
        P(("ctx", "head"), None),
        P(("ctx", "head"), None),
        P("ctx", "head"),
        P(),
        P(),
    )
    return jax.shard_map(
        shards,
        mesh=mesh,
        in_specs=placed,
        out_specs=(
            P("ctx", "head"),
            P(("ctx", "head"), None),
            P(("ctx", "head"), None),
            P(("ctx", "head"), None),
        ),
        check_vma=False,
    )
```

```python
import functools
import math

import jax
import jax.numpy as jnp
from jax import lax
from jax.experimental import pallas as pl
from jax.experimental.pallas import tpu as pltpu
from jax.sharding import PartitionSpec as P

MESH = pl.DeviceIdType.MESH
BF16 = jnp.bfloat16
F32 = jnp.float32

N_CTX, N_HEAD = 32, 4
NZ, NY, NCORE = 4, 4, 2
PLANE = NY * NCORE
PLANES = 3
SLOTS = 9
PAIR = 256
TOK = 128
PART = 32
DIM = 128
GROUP = 8
ROWS = TOK * GROUP
COLS = GROUP * DIM
NDOCS = 16
MASKED = -1e30
SCALE = 1.0 / math.sqrt(DIM)
LOG2E = 1.0 / math.log(2.0)

XQ, G1, G2, A1, A2, DQ = range(6)
X0, X1, X2, Y1, YV, C1, CV, YP, XPV, XP, CP = (6, 8, 10, 12, 14, 16, 18, 20, 22, 24, 30)
N_SEM = 36
LK, LV, LQ, LG, LS, LA = range(6)
N_LOCAL = 6


def body(
    q_in, k_in, v_in, go_in, owned, doc_lengths,
    ao, gq, gk, gv,
    kv, qs, gcol, gperm, gos, acol, aperm, out_rows, dq_rows,
    q_rows, q_cols, go_cols, probs, rounded_probs, parts, from_core, y_sum, from_y, sums, from_x,
    slot_vec, slot_of, send, recv, local,
):
    c = lax.axis_index("ctx")
    h = lax.axis_index("head")
    z = c // PLANE
    idx = lax.rem(c, PLANE)
    y = idx // NCORE
    co = lax.rem(idx, NCORE)
    sib = c + 1 - 2 * co
    tile_row = pl.multiple_of(16 * (c // GROUP), 16)
    tile_head = lax.rem(c, GROUP)

    def ctx_at(zz, yy):
        return lax.rem(zz, NZ) * PLANE + lax.rem(yy, NY) * NCORE + co

    def push(src, dst, sem, ctx, head):
        copy = pltpu.make_async_remote_copy(
            src_ref=src, dst_ref=dst, send_sem=send.at[sem], recv_sem=recv.at[sem],
            device_id=(ctx, head), device_id_type=MESH,
        )
        copy.start()

    def drain(ref, sem):
        pltpu.make_async_copy(ref, ref, sem).wait()

    def cols(number, width):
        return pl.ds(pl.multiple_of(number * width, width), width)

    own_slot = NY + y

    local_copies = [
        pltpu.make_async_copy(k_in.at[:, cols(h, DIM)], kv.at[0, own_slot, co, cols(h, PART), :], local.at[LK]),
        pltpu.make_async_copy(v_in.at[:, cols(h, DIM)], kv.at[1, own_slot, co, cols(h, PART), :], local.at[LV]),
        pltpu.make_async_copy(q_in.at[:, cols(h, COLS)], qs.at[cols(h, PART), :], local.at[LQ]),
        pltpu.make_async_copy(
            go_in.at[:, pl.ds(tile_row, 16), cols(tile_head, DIM)], gcol.at[pl.ds(2 * c, 2)], local.at[LG]
        ),
    ]
    for copy in local_copies:
        copy.start()

    barrier = pltpu.get_barrier_semaphore()

    def greet(step, carry):
        pl.semaphore_signal(barrier, inc=1, device_id=(lax.rem(c + step, N_CTX), h), device_id_type=MESH)
        return carry

    lax.fori_loop(1, N_CTX, greet, 0)
    def greet_heads(ctx):
        for step in range(1, N_HEAD):
            pl.semaphore_signal(barrier, inc=1, device_id=(ctx, lax.rem(h + step, N_HEAD)), device_id_type=MESH)

    for ahead in range(NZ):
        greet_heads(ctx_at(z + ahead, y))

    pl.semaphore_wait(barrier, N_CTX - 1 + NZ * (N_HEAD - 1))

    def tile_of(number):
        return pl.multiple_of(16 * (number // GROUP), 16), lax.rem(number, GROUP)

    def collect_grad(step, carry):
        to = lax.rem(c + step, N_CTX)
        row, head = tile_of(to)
        push(go_in.at[:, pl.ds(row, 16), cols(head, DIM)], gcol.at[pl.ds(2 * c, 2)], G1, to, h)
        return carry


    def by_head(which, slot, sem, ctx, first_step):
        for step in range(first_step, N_HEAD):
            to = lax.rem(h + step, N_HEAD)
            push(
                (k_in, v_in)[which].at[:, cols(to, DIM)], kv.at[which, slot, co, cols(h, PART), :], sem + which, ctx, to
            )

    def first_hop(which):
        by_head(which, own_slot, X0, c, 1)
        by_head(which, y, X1, ctx_at(z + 1, y), 0)
        by_head(which, 2 * NY, X2, ctx_at(z + 2, y), 0)

    first_hop(0)
    for step in range(1, N_HEAD):
        to = lax.rem(h + step, N_HEAD)
        push(q_in.at[:, cols(to, COLS)], qs.at[cols(h, PART), :], XQ, c, to)
    first_hop(1)
    lax.fori_loop(1, N_CTX, collect_grad, 0)

    def along_y(which):
        drain(kv.at[0, 0, 0, pl.ds(0, 3 * PART), :], recv.at[X0 + which])
        for step in range(1, NY):
            yy = lax.rem(y + step, NY)

            @pl.when(yy > y)
            def _():
                push(kv.at[which, own_slot, co], kv.at[which, own_slot, co], YV + which, ctx_at(z, yy), h)

        drain(kv.at[0, 0, 0], recv.at[X1 + which])
        for step in range(1, NY):
            push(kv.at[which, y, co], kv.at[which, y, co], Y1 + which, ctx_at(z, y + step), h)
        drain(kv.at[0, 0, 0], recv.at[X2 + which])
        for step in range(1, NY):
            yy = lax.rem(y + step, NY)

            @pl.when(yy < y)
            def _():
                push(kv.at[which, 2 * NY, co], kv.at[which, own_slot, co], YV + which, ctx_at(z, yy), h)

    lanes = lax.broadcasted_iota(jnp.int32, (8, DIM), 1)
    found = jnp.zeros((8, DIM), jnp.int32)
    for number in range(2 * N_CTX):
        found = jnp.where(lanes == owned[number % 2, number // 2], number, found)
    slot_vec[...] = found
    slot_copy = pltpu.make_async_copy(slot_vec, slot_of, local.at[LS])
    slot_copy.start()

    local_copies[0].wait()
    along_y(0)
    local_copies[1].wait()
    along_y(1)

    q_pos = c * TOK + lax.broadcasted_iota(jnp.int32, (1, TOK), 1)
    first = jnp.zeros((1, TOK), jnp.int32)
    begin = jnp.int32(0)
    for doc in range(NDOCS):
        first = jnp.where(q_pos >= begin, jnp.maximum(first, begin), first)
        begin = begin + doc_lengths[doc]

    local_copies[3].wait()
    slot_copy.wait()
    drain(gcol.at[pl.ds(0, 62)], recv.at[G1])

    def arrange_grad(number, carry):
        gperm[number] = gcol[slot_of[0, number]]
        return carry

    lax.fori_loop(0, 2 * N_CTX, arrange_grad, 0, unroll=8)

    def deliver_grad(step, carry):
        to = lax.rem(c + step, N_CTX)
        push(
            gperm.at[pl.ds(2 * to, 2)], gos.at[tile_head, :, pl.ds(tile_row, 16), :], G2, to, h
        )
        return carry

    lax.fori_loop(1, N_CTX, deliver_grad, 0)
    gos[tile_head, :, pl.ds(tile_row, 16), :] = gperm[pl.ds(2 * c, 2)]

    local_copies[2].wait()
    drain(qs.at[pl.ds(0, 3 * PART), :], recv.at[XQ])
    for head in range(GROUP):
        rows = qs[:, head * DIM : (head + 1) * DIM]
        q_rows[head * TOK : (head + 1) * TOK, :] = rows
        q_cols[:, head * TOK : (head + 1) * TOK] = rows.T

    def to_other_core(which):
        drain(kv.at[0, pl.ds(0, 3), 0], recv.at[Y1 + which])
        push(kv.at[which, pl.ds(0, NY), co], kv.at[which, pl.ds(0, NY), co], C1 + which, sib, h)
        drain(kv.at[0, pl.ds(0, 3), 0], recv.at[YV + which])
        push(kv.at[which, pl.ds(NY, NY + 1), co], kv.at[which, pl.ds(NY, NY + 1), co], CV + which, sib, h)

    to_other_core(0)

    def position(slot):
        if slot < NY:
            return ((z - 1) * NY + slot) * PAIR
        if slot < 2 * NY:
            return (jnp.where(slot - NY <= y, z, z - 2) * NY + slot - NY) * PAIR
        return ((z - 2) * NY + y) * PAIR

    def scores(slot, peak):
        keys = kv[0, slot].reshape(PAIR, DIM)
        key_pos = position(slot) + lax.broadcasted_iota(jnp.int32, (PAIR, TOK), 0)
        bias = jnp.where((key_pos <= q_pos) & (key_pos >= first), 0.0, MASKED)
        bias = jnp.concatenate([bias] * GROUP, axis=1)
        block = jnp.dot(keys, q_cols[...], preferred_element_type=F32) * (SCALE * LOG2E) + bias
        probs[slot] = block
        return jnp.maximum(peak, jnp.max(block.reshape(PAIR // 8, 8, ROWS), axis=0))

    peak = jnp.full((8, ROWS), MASKED, F32)
    drain(kv.at[0, pl.ds(0, NY), 0], recv.at[C1])
    for slot in range(NY):
        peak = scores(slot, peak)
    drain(kv.at[0, pl.ds(0, NY + 1), 0], recv.at[CV])
    for slot in range(NY, SLOTS):
        peak = scores(slot, peak)
    peak = jnp.max(peak, axis=0, keepdims=True)
    to_other_core(1)

    total = jnp.zeros((8, ROWS), F32)
    for slot in range(SLOTS):
        block = jnp.exp2(probs[slot] - peak)
        probs[slot] = block
        rounded_probs[slot] = block.astype(BF16)
        total = total + jnp.sum(block.reshape(PAIR // 8, 8, ROWS), axis=0)
    drain(kv.at[0, pl.ds(0, NY), 0], recv.at[C1 + 1])
    drain(kv.at[0, pl.ds(0, NY + 1), 0], recv.at[CV + 1])
    accum = jnp.zeros((DIM, ROWS), F32)
    for slot in range(SLOTS):
        values = kv[1, slot].reshape(PAIR, DIM)
        accum = accum + jnp.dot(values.T, rounded_probs[slot], preferred_element_type=F32)
    inverse = 1.0 / jnp.sum(total, axis=0, keepdims=True)
    rounded = (accum * inverse).astype(BF16)
    for head in range(GROUP):
        rows = rounded[:, head * TOK : (head + 1) * TOK].T
        out_rows[head, 0] = rows[:64]
        out_rows[head, 1] = rows[64:]

    def collect_out(step, carry):
        to = lax.rem(c + step, N_CTX)
        row, head = tile_of(to)
        push(out_rows.at[head, :, pl.ds(row, 16), :], acol.at[pl.ds(2 * c, 2)], A1, to, h)
        return carry

    lax.fori_loop(1, N_CTX, collect_out, 0)
    acol[pl.ds(2 * c, 2)] = out_rows[tile_head, :, pl.ds(tile_row, 16), :]

    drain(gperm.at[pl.ds(0, 62)], recv.at[G2])
    for head in range(GROUP):
        go_cols[:, head * TOK : (head + 1) * TOK] = gos[head].reshape(TOK, DIM).T
    delta = jnp.sum(go_cols[...].astype(F32) * rounded.astype(F32), axis=0, keepdims=True)

    beside = [lax.rem(y + step, NY) for step in range(1, NY)]
    virtual = [NY + yy for yy in beside]
    rest = [y, 2 * NY, own_slot]

    def both_cores(which, slot):
        return parts[which, slot, co].astype(F32) + from_core[which, slot].astype(F32)

    def home(which, number, sem, ctx, first_step):
        for step in range(first_step, N_HEAD):
            to = lax.rem(h + step, N_HEAD)
            push(sums.at[which, number, cols(to, PART), :], from_x.at[which, number, h], sem, ctx, to)

    def beside_home(which):
        for step, slot in enumerate(beside):
            y_sum[which, step] = both_cores(which, slot).astype(BF16)
            push(y_sum.at[which, step], from_y.at[which, step], YP + which, ctx_at(z, y + step + 1), h)

    def virtual_home(which):
        for step, slot in enumerate(virtual):
            sums[which, PLANES + step] = both_cores(which, slot).astype(BF16)
            plane = jnp.where(beside[step] <= y, z, z + 2)
            home(which, PLANES + step, XPV + which, ctx_at(plane, beside[step]), 0)

    def rest_home(which):
        sums[which, 0] = both_cores(which, 2 * NY).astype(BF16)
        home(which, 0, XP + 3 * which, ctx_at(z + 2, y), 0)
        sums[which, 2] = both_cores(which, own_slot).astype(BF16)
        home(which, 2, XP + 3 * which + 2, c, 1)
        from_x[which, 2, h] = sums[which, 2, cols(h, PART), :]

    def before_home(which):
        drain(from_y.at[0], recv.at[YP + which])
        before = both_cores(which, y)
        for step in range(NY - 1):
            before = before + from_y[which, step].astype(F32)
        sums[which, 1] = before.astype(BF16)
        home(which, 1, XP + 3 * which + 1, ctx_at(z + 3, y), 0)

    def value_group(slots, sem):
        for slot in slots:
            weights = (probs[slot] * inverse).astype(BF16)
            part = jnp.dot(weights, gos[...].reshape(ROWS, DIM), preferred_element_type=F32)
            parts[1, slot] = part.astype(BF16).reshape(NCORE, TOK, DIM)
        for slot in slots:
            push(parts.at[1, slot, 1 - co], from_core.at[1, slot], sem, sib, h)

    def key_group(slots, sem, query_grad):
        for slot in slots:
            keys, values = kv[0, slot].reshape(PAIR, DIM), kv[1, slot].reshape(PAIR, DIM)
            pushed = jnp.dot(values, go_cols[...], preferred_element_type=F32)
            slopes = (probs[slot] * inverse * (pushed - delta)).astype(BF16)
            part = jnp.dot(slopes, q_rows[...], preferred_element_type=F32) * SCALE
            parts[0, slot] = part.astype(BF16).reshape(NCORE, TOK, DIM)
            query_grad = query_grad + jnp.dot(keys.T, slopes, preferred_element_type=F32)
        for slot in slots:
            push(parts.at[0, slot, 1 - co], from_core.at[0, slot], sem, sib, h)
        return query_grad

    def drain_core(sem):
        drain(from_core.at[0, pl.ds(0, 3)], recv.at[sem])

    value_group(beside, CP)
    value_group(virtual, CP + 1)
    value_group(rest, CP + 2)
    query_grad = jnp.zeros((DIM, ROWS), F32)
    query_grad = key_group(beside, CP + 3, query_grad)
    drain_core(CP)
    beside_home(1)
    drain_core(CP + 1)
    virtual_home(1)
    drain_core(CP + 2)
    rest_home(1)
    query_grad = key_group(virtual, CP + 4, query_grad)
    drain_core(CP + 3)
    beside_home(0)
    query_grad = key_group(rest, CP + 5, query_grad)
    drain_core(CP + 4)
    virtual_home(0)

    query_grad = (query_grad * SCALE).astype(BF16)
    for head in range(GROUP):
        dq_rows[:, head * DIM : (head + 1) * DIM] = query_grad[:, head * TOK : (head + 1) * TOK].T
    for step in range(1, N_HEAD):
        to = lax.rem(h + step, N_HEAD)
        push(dq_rows.at[cols(to, PART), :], gq.at[:, cols(h, COLS)], DQ, c, to)
    gq[:, cols(h, COLS)] = dq_rows[cols(h, PART), :]

    drain(acol.at[pl.ds(0, 62)], recv.at[A1])

    def arrange_out(number, carry):
        aperm[2 * number] = acol[owned[0, number]]
        aperm[2 * number + 1] = acol[owned[1, number]]
        return carry

    lax.fori_loop(0, N_CTX, arrange_out, 0, unroll=4)

    def deliver_out(step, carry):
        to = lax.rem(c + step, N_CTX)
        push(
            aperm.at[pl.ds(2 * to, 2)], ao.at[:, pl.ds(tile_row, 16), cols(tile_head, DIM)], A2, to, h
        )
        return carry

    lax.fori_loop(1, N_CTX, deliver_out, 0)
    own_out = pltpu.make_async_copy(
        aperm.at[pl.ds(2 * c, 2)], ao.at[:, pl.ds(tile_row, 16), cols(tile_head, DIM)], local.at[LA]
    )
    own_out.start()
    drain_core(CP + 5)
    rest_home(0)
    before_home(1)
    before_home(0)

    for which in (1, 0):
        drain(from_x.at[0, pl.ds(PLANES, 3)], recv.at[XPV + which])
        drain(from_x.at[0, 0], recv.at[XP + 3 * which])
        drain(from_x.at[0, 0, pl.ds(0, 3)], recv.at[XP + 3 * which + 2])
        drain(from_x.at[0, 0], recv.at[XP + 3 * which + 1])
        for head in range(N_HEAD):
            piece = from_x[which, 0, head].astype(F32)
            for number in range(1, PLANES + NY - 1):
                piece = piece + from_x[which, number, head].astype(F32)
            (gk, gv)[which][:, head * DIM : (head + 1) * DIM] = piece.astype(BF16)
    three_cols = pl.ds(0, 3 * COLS)
    drain(gperm.at[pl.ds(0, 62)], recv.at[A2])
    drain(gq.at[:, three_cols], recv.at[DQ])
    own_out.wait()
    for sem in (G1, G2, A1, A2):
        drain(gperm.at[pl.ds(0, 62)], send.at[sem])
    for sem in (XQ, DQ):
        drain(gq.at[:, three_cols], send.at[sem])
    for which in range(2):
        for sem in (X0 + which, XP + 3 * which + 2):
            drain(from_x.at[0, 0, pl.ds(0, 3)], send.at[sem])
        for sem in (X1 + which, X2 + which, XP + 3 * which, XP + 3 * which + 1):
            drain(from_x.at[0, 0], send.at[sem])
        for sem in (Y1, YV, YP, XPV):
            drain(from_y.at[0], send.at[sem + which])
        for sem in range(3):
            drain(from_y.at[0], send.at[CP + 3 * which + sem])
        drain(kv.at[0, pl.ds(0, NY), 0], send.at[C1 + which])
        drain(kv.at[0, pl.ds(0, NY + 1), 0], send.at[CV + which])


def finish_body(ao, gq, gk, gv, ao_out, gq_out, gk_out, gv_out, sems):
    copies = [
        pltpu.make_async_copy(src, dst, sems.at[number])
        for number, (src, dst) in enumerate(((ao, ao_out), (gq, gq_out), (gk, gk_out), (gv, gv_out)))
    ]
    for copy in copies:
        copy.start()
    for copy in copies:
        copy.wait()


def finish(*arrays):
    anywhere = pl.BlockSpec(memory_space=pltpu.VMEM)
    arrays = [pltpu.with_memory_space_constraint(array, pltpu.VMEM) for array in arrays]
    hbm = pl.BlockSpec(memory_space=pltpu.HBM)
    return pl.pallas_call(
        finish_body,
        out_shape=tuple(jax.ShapeDtypeStruct(array.shape, array.dtype) for array in arrays),
        in_specs=[anywhere] * 4,
        out_specs=(hbm,) * 4,
        scratch_shapes=[pltpu.SemaphoreType.DMA((4,))],
        name="write_outputs",
    )(*arrays)


def shards(queries, keys, values, grad_out, owner_lists, doc_lengths):
    hbm = pl.BlockSpec(memory_space=pltpu.HBM)
    smem = pl.BlockSpec(memory_space=pltpu.SMEM)
    block = (TOK, DIM)
    ao, gq, gk, gv = pl.pallas_call(
        body,
        out_shape=(
            pltpu.VMEM((2, TOK // 2, COLS), BF16),
            pltpu.VMEM((PART, N_HEAD * COLS), BF16),
            pltpu.VMEM((PART, N_HEAD * DIM), BF16),
            pltpu.VMEM((PART, N_HEAD * DIM), BF16),
        ),
        in_specs=[hbm] * 4 + [smem] * 2,
        out_specs=(pl.BlockSpec(memory_space=pltpu.VMEM),) * 4,
        scratch_shapes=[
            pltpu.VMEM((2, SLOTS, NCORE) + block, BF16),
            pltpu.VMEM((TOK, COLS), BF16),
            pltpu.VMEM((2 * N_CTX, 16, DIM), BF16),
            pltpu.VMEM((2 * N_CTX, 16, DIM), BF16),
            pltpu.VMEM((GROUP, 2, TOK // 2, DIM), BF16),
            pltpu.VMEM((2 * N_CTX, 16, DIM), BF16),
            pltpu.VMEM((2 * N_CTX, 16, DIM), BF16),
            pltpu.VMEM((GROUP, 2, TOK // 2, DIM), BF16),
            pltpu.VMEM((TOK, COLS), BF16),
            pltpu.VMEM((ROWS, DIM), BF16),
            pltpu.VMEM((DIM, ROWS), BF16),
            pltpu.VMEM((DIM, ROWS), BF16),
            pltpu.VMEM((SLOTS, PAIR, ROWS), F32),
            pltpu.VMEM((SLOTS, PAIR, ROWS), BF16),
            pltpu.VMEM((2, SLOTS, NCORE) + block, BF16),
            pltpu.VMEM((2, SLOTS) + block, BF16),
            pltpu.VMEM((2, NY - 1) + block, BF16),
            pltpu.VMEM((2, NY - 1) + block, BF16),
            pltpu.VMEM((2, PLANES + NY - 1) + block, BF16),
            pltpu.VMEM((2, PLANES + NY - 1, N_HEAD, PART, DIM), BF16),
            pltpu.VMEM((8, DIM), jnp.int32),
            pltpu.SMEM((8, DIM), jnp.int32),
            pltpu.SemaphoreType.DMA((N_SEM,)),
            pltpu.SemaphoreType.DMA((N_SEM,)),
            pltpu.SemaphoreType.DMA((N_LOCAL,)),
        ],
        compiler_params=pltpu.CompilerParams(
            collective_id=0, has_side_effects=True, vmem_limit_bytes=56 * 1024 * 1024
        ),
        cost_estimate=pl.CostEstimate(flops=4_000_000_000, bytes_accessed=4_000_000, transcendentals=2_300_000),
        name="attention_core",
    )(queries, keys, values, grad_out.reshape(2, TOK // 2, COLS), owner_lists.T, doc_lengths)
    return finish(ao.reshape(TOK, COLS), gq, gk, gv)


def solution(mesh):
    placed = (
        P(("ctx", "head"), None),
        P(("ctx", "head"), None),
        P(("ctx", "head"), None),
        P("ctx", "head"),
        P(),
        P(),
    )
    return jax.shard_map(
        shards,
        mesh=mesh,
        in_specs=placed,
        out_specs=(
            P("ctx", "head"),
            P(("ctx", "head"), None),
            P(("ctx", "head"), None),
            P(("ctx", "head"), None),
        ),
        check_vma=False,
    )
```

```python
import functools
import math

import jax
import jax.numpy as jnp
from jax import lax
from jax.experimental import pallas as pl
from jax.experimental.pallas import tpu as pltpu
from jax.sharding import PartitionSpec as P

MESH = pl.DeviceIdType.MESH
BF16 = jnp.bfloat16
F32 = jnp.float32

N_CTX, N_HEAD = 32, 4
NZ, NY, NCORE = 4, 4, 2
PLANE = NY * NCORE
PLANES = 3
SLOTS = 9
PAIR = 256
TOK = 128
PART = 32
DIM = 128
GROUP = 8
ROWS = TOK * GROUP
COLS = GROUP * DIM
NDOCS = 16
MASKED = -1e30
SCALE = 1.0 / math.sqrt(DIM)
LOG2E = 1.0 / math.log(2.0)

XQ, G1, G2, A1, A2, DQ = range(6)
X0, X1, X2, Y1, YV, C1, CV, YP, XPV, XP, CP = (6, 8, 10, 12, 14, 16, 18, 20, 22, 24, 30)
N_SEM = 36
LK, LV, LQ, LG, LS, LA = range(6)
N_LOCAL = 6


def body(
    q_in, k_in, v_in, go_in, owned, doc_lengths,
    ao, gq, gk, gv,
    kv, qs, gcol, gperm, gos, acol, aperm, out_rows, dq_rows,
    q_rows, q_cols, go_cols, probs, rounded_probs, parts, from_core, y_sum, from_y, sums, from_x,
    slot_vec, slot_of, send, recv, local,
):
    c = lax.axis_index("ctx")
    h = lax.axis_index("head")
    z = c // PLANE
    idx = lax.rem(c, PLANE)
    y = idx // NCORE
    co = lax.rem(idx, NCORE)
    sib = c + 1 - 2 * co
    tile_row = pl.multiple_of(16 * (c // GROUP), 16)
    tile_head = lax.rem(c, GROUP)

    def ctx_at(zz, yy):
        return lax.rem(zz, NZ) * PLANE + lax.rem(yy, NY) * NCORE + co

    def push(src, dst, sem, ctx, head):
        copy = pltpu.make_async_remote_copy(
            src_ref=src, dst_ref=dst, send_sem=send.at[sem], recv_sem=recv.at[sem],
            device_id=(ctx, head), device_id_type=MESH,
        )
        copy.start()

    def drain(ref, sem):
        pltpu.make_async_copy(ref, ref, sem).wait()

    def cols(number, width):
        return pl.ds(pl.multiple_of(number * width, width), width)

    own_slot = NY + y

    local_copies = [
        pltpu.make_async_copy(k_in.at[:, cols(h, DIM)], kv.at[0, own_slot, co, cols(h, PART), :], local.at[LK]),
        pltpu.make_async_copy(v_in.at[:, cols(h, DIM)], kv.at[1, own_slot, co, cols(h, PART), :], local.at[LV]),
        pltpu.make_async_copy(q_in.at[:, cols(h, COLS)], qs.at[cols(h, PART), :], local.at[LQ]),
        pltpu.make_async_copy(
            go_in.at[:, pl.ds(tile_row, 16), cols(tile_head, DIM)], gcol.at[pl.ds(2 * c, 2)], local.at[LG]
        ),
    ]
    for copy in local_copies:
        copy.start()

    barrier = pltpu.get_barrier_semaphore()

    def greet(step, carry):
        pl.semaphore_signal(barrier, inc=1, device_id=(lax.rem(c + step, N_CTX), h), device_id_type=MESH)
        return carry

    lax.fori_loop(1, N_CTX, greet, 0)
    def greet_heads(ctx):
        for step in range(1, N_HEAD):
            pl.semaphore_signal(barrier, inc=1, device_id=(ctx, lax.rem(h + step, N_HEAD)), device_id_type=MESH)

    for ahead in range(NZ):
        greet_heads(ctx_at(z + ahead, y))

    pl.semaphore_wait(barrier, N_CTX - 1 + NZ * (N_HEAD - 1))

    def tile_of(number):
        return pl.multiple_of(16 * (number // GROUP), 16), lax.rem(number, GROUP)

    def collect_grad(step, carry):
        to = lax.rem(c + step, N_CTX)
        row, head = tile_of(to)
        push(go_in.at[:, pl.ds(row, 16), cols(head, DIM)], gcol.at[pl.ds(2 * c, 2)], G1, to, h)
        return carry


    def by_head(which, slot, sem, ctx, first_step):
        for step in range(first_step, N_HEAD):
            to = lax.rem(h + step, N_HEAD)
            push(
                (k_in, v_in)[which].at[:, cols(to, DIM)], kv.at[which, slot, co, cols(h, PART), :], sem + which, ctx, to
            )

    def first_hop(which):
        by_head(which, own_slot, X0, c, 1)
        by_head(which, y, X1, ctx_at(z + 1, y), 0)
        by_head(which, 2 * NY, X2, ctx_at(z + 2, y), 0)

    first_hop(0)
    for step in range(1, N_HEAD):
        to = lax.rem(h + step, N_HEAD)
        push(q_in.at[:, cols(to, COLS)], qs.at[cols(h, PART), :], XQ, c, to)
    first_hop(1)
    lax.fori_loop(1, N_CTX, collect_grad, 0)

    def along_y(which):
        drain(kv.at[0, 0, 0, pl.ds(0, 3 * PART), :], recv.at[X0 + which])
        for step in range(1, NY):
            yy = lax.rem(y + step, NY)

            @pl.when(yy > y)
            def _():
                push(kv.at[which, own_slot, co], kv.at[which, own_slot, co], YV + which, ctx_at(z, yy), h)

        drain(kv.at[0, 0, 0], recv.at[X1 + which])
        for step in range(1, NY):
            push(kv.at[which, y, co], kv.at[which, y, co], Y1 + which, ctx_at(z, y + step), h)
        drain(kv.at[0, 0, 0], recv.at[X2 + which])
        for step in range(1, NY):
            yy = lax.rem(y + step, NY)

            @pl.when(yy < y)
            def _():
                push(kv.at[which, 2 * NY, co], kv.at[which, own_slot, co], YV + which, ctx_at(z, yy), h)

    lanes = lax.broadcasted_iota(jnp.int32, (8, DIM), 1)
    found = jnp.zeros((8, DIM), jnp.int32)
    for number in range(2 * N_CTX):
        found = jnp.where(lanes == owned[number % 2, number // 2], number, found)
    slot_vec[...] = found
    slot_copy = pltpu.make_async_copy(slot_vec, slot_of, local.at[LS])
    slot_copy.start()

    local_copies[0].wait()
    along_y(0)
    local_copies[1].wait()
    along_y(1)

    q_pos = c * TOK + lax.broadcasted_iota(jnp.int32, (1, TOK), 1)
    first = jnp.zeros((1, TOK), jnp.int32)
    begin = jnp.int32(0)
    for doc in range(NDOCS):
        first = jnp.where(q_pos >= begin, jnp.maximum(first, begin), first)
        begin = begin + doc_lengths[doc]

    local_copies[3].wait()
    slot_copy.wait()
    drain(gcol.at[pl.ds(0, 62)], recv.at[G1])

    def arrange_grad(number, carry):
        gperm[number] = gcol[slot_of[0, number]]
        return carry

    lax.fori_loop(0, 2 * N_CTX, arrange_grad, 0, unroll=8)

    def deliver_grad(step, carry):
        to = lax.rem(c + step, N_CTX)
        push(
            gperm.at[pl.ds(2 * to, 2)], gos.at[tile_head, :, pl.ds(tile_row, 16), :], G2, to, h
        )
        return carry

    lax.fori_loop(1, N_CTX, deliver_grad, 0)
    gos[tile_head, :, pl.ds(tile_row, 16), :] = gperm[pl.ds(2 * c, 2)]

    local_copies[2].wait()
    drain(qs.at[pl.ds(0, 3 * PART), :], recv.at[XQ])
    for head in range(GROUP):
        rows = qs[:, head * DIM : (head + 1) * DIM]
        q_rows[head * TOK : (head + 1) * TOK, :] = rows
        q_cols[:, head * TOK : (head + 1) * TOK] = rows.T

    def to_other_core(which):
        drain(kv.at[0, pl.ds(0, 3), 0], recv.at[Y1 + which])
        push(kv.at[which, pl.ds(0, NY), co], kv.at[which, pl.ds(0, NY), co], C1 + which, sib, h)
        drain(kv.at[0, pl.ds(0, 3), 0], recv.at[YV + which])
        push(kv.at[which, pl.ds(NY, NY + 1), co], kv.at[which, pl.ds(NY, NY + 1), co], CV + which, sib, h)

    to_other_core(0)

    def position(slot):
        if slot < NY:
            return ((z - 1) * NY + slot) * PAIR
        if slot < 2 * NY:
            return (jnp.where(slot - NY <= y, z, z - 2) * NY + slot - NY) * PAIR
        return ((z - 2) * NY + y) * PAIR

    def scores(slot, peak):
        keys = kv[0, slot].reshape(PAIR, DIM)
        key_pos = position(slot) + lax.broadcasted_iota(jnp.int32, (PAIR, TOK), 0)
        bias = jnp.where((key_pos <= q_pos) & (key_pos >= first), 0.0, MASKED)
        bias = jnp.concatenate([bias] * GROUP, axis=1)
        block = jnp.dot(keys, q_cols[...], preferred_element_type=F32) * (SCALE * LOG2E) + bias
        probs[slot] = block
        return jnp.maximum(peak, jnp.max(block.reshape(PAIR // 8, 8, ROWS), axis=0))

    peak = jnp.full((8, ROWS), MASKED, F32)
    drain(kv.at[0, pl.ds(0, NY), 0], recv.at[C1])
    for slot in range(NY):
        peak = scores(slot, peak)
    drain(kv.at[0, pl.ds(0, NY + 1), 0], recv.at[CV])
    for slot in range(NY, SLOTS):
        peak = scores(slot, peak)
    peak = jnp.max(peak, axis=0, keepdims=True)
    to_other_core(1)

    total = jnp.zeros((8, ROWS), F32)
    for slot in range(SLOTS):
        block = jnp.exp2(probs[slot] - peak)
        probs[slot] = block
        rounded_probs[slot] = block.astype(BF16)
        total = total + jnp.sum(block.reshape(PAIR // 8, 8, ROWS), axis=0)
    drain(kv.at[0, pl.ds(0, NY), 0], recv.at[C1 + 1])
    drain(kv.at[0, pl.ds(0, NY + 1), 0], recv.at[CV + 1])
    accum = jnp.zeros((DIM, ROWS), F32)
    for slot in range(SLOTS):
        values = kv[1, slot].reshape(PAIR, DIM)
        accum = accum + jnp.dot(values.T, rounded_probs[slot], preferred_element_type=F32)
    inverse = 1.0 / jnp.sum(total, axis=0, keepdims=True)
    rounded = (accum * inverse).astype(BF16)
    for head in range(GROUP):
        rows = rounded[:, head * TOK : (head + 1) * TOK].T
        out_rows[head, 0] = rows[:64]
        out_rows[head, 1] = rows[64:]

    def collect_out(step, carry):
        to = lax.rem(c + step, N_CTX)
        row, head = tile_of(to)
        push(out_rows.at[head, :, pl.ds(row, 16), :], acol.at[pl.ds(2 * c, 2)], A1, to, h)
        return carry

    lax.fori_loop(1, N_CTX, collect_out, 0)
    acol[pl.ds(2 * c, 2)] = out_rows[tile_head, :, pl.ds(tile_row, 16), :]

    drain(gperm.at[pl.ds(0, 62)], recv.at[G2])
    for head in range(GROUP):
        go_cols[:, head * TOK : (head + 1) * TOK] = gos[head].reshape(TOK, DIM).T
    delta = jnp.sum(go_cols[...].astype(F32) * rounded.astype(F32), axis=0, keepdims=True)

    beside = [lax.rem(y + step, NY) for step in range(1, NY)]
    virtual = [NY + yy for yy in beside]
    rest = [y, 2 * NY, own_slot]

    def both_cores(which, slot):
        return parts[which, slot, co].astype(F32) + from_core[which, slot].astype(F32)

    def home(which, number, sem, ctx, first_step):
        for step in range(first_step, N_HEAD):
            to = lax.rem(h + step, N_HEAD)
            push(sums.at[which, number, cols(to, PART), :], from_x.at[which, number, h], sem, ctx, to)

    def beside_home(which):
        for step, slot in enumerate(beside):
            y_sum[which, step] = both_cores(which, slot).astype(BF16)
            push(y_sum.at[which, step], from_y.at[which, step], YP + which, ctx_at(z, y + step + 1), h)

    def virtual_home(which):
        for step, slot in enumerate(virtual):
            sums[which, PLANES + step] = both_cores(which, slot).astype(BF16)
            plane = jnp.where(beside[step] <= y, z, z + 2)
            home(which, PLANES + step, XPV + which, ctx_at(plane, beside[step]), 0)

    def rest_home(which):
        sums[which, 0] = both_cores(which, 2 * NY).astype(BF16)
        home(which, 0, XP + 3 * which, ctx_at(z + 2, y), 0)
        sums[which, 2] = both_cores(which, own_slot).astype(BF16)
        home(which, 2, XP + 3 * which + 2, c, 1)
        from_x[which, 2, h] = sums[which, 2, cols(h, PART), :]

    def before_home(which):
        drain(from_y.at[0], recv.at[YP + which])
        before = both_cores(which, y)
        for step in range(NY - 1):
            before = before + from_y[which, step].astype(F32)
        sums[which, 1] = before.astype(BF16)
        home(which, 1, XP + 3 * which + 1, ctx_at(z + 3, y), 0)

    def value_group(slots, sem):
        for slot in slots:
            weights = (probs[slot] * inverse).astype(BF16)
            part = jnp.dot(weights, gos[...].reshape(ROWS, DIM), preferred_element_type=F32)
            parts[1, slot] = part.astype(BF16).reshape(NCORE, TOK, DIM)
        for slot in slots:
            push(parts.at[1, slot, 1 - co], from_core.at[1, slot], sem, sib, h)

    def key_group(slots, sem, query_grad):
        for slot in slots:
            keys, values = kv[0, slot].reshape(PAIR, DIM), kv[1, slot].reshape(PAIR, DIM)
            pushed = jnp.dot(values, go_cols[...], preferred_element_type=F32)
            slopes = (probs[slot] * inverse * (pushed - delta)).astype(BF16)
            part = jnp.dot(slopes, q_rows[...], preferred_element_type=F32) * SCALE
            parts[0, slot] = part.astype(BF16).reshape(NCORE, TOK, DIM)
            query_grad = query_grad + jnp.dot(keys.T, slopes, preferred_element_type=F32)
        for slot in slots:
            push(parts.at[0, slot, 1 - co], from_core.at[0, slot], sem, sib, h)
        return query_grad

    def drain_core(sem):
        drain(from_core.at[0, pl.ds(0, 3)], recv.at[sem])

    value_group(beside, CP)
    value_group(virtual, CP + 1)
    value_group(rest, CP + 2)
    query_grad = jnp.zeros((DIM, ROWS), F32)
    query_grad = key_group(beside, CP + 3, query_grad)
    drain_core(CP)
    beside_home(1)
    drain_core(CP + 1)
    virtual_home(1)
    drain_core(CP + 2)
    rest_home(1)
    query_grad = key_group(virtual, CP + 4, query_grad)
    drain_core(CP + 3)
    beside_home(0)
    query_grad = key_group(rest, CP + 5, query_grad)
    drain_core(CP + 4)
    virtual_home(0)

    query_grad = (query_grad * SCALE).astype(BF16)
    for head in range(GROUP):
        dq_rows[:, head * DIM : (head + 1) * DIM] = query_grad[:, head * TOK : (head + 1) * TOK].T
    for step in range(1, N_HEAD):
        to = lax.rem(h + step, N_HEAD)
        push(dq_rows.at[cols(to, PART), :], gq.at[:, cols(h, COLS)], DQ, c, to)
    gq[:, cols(h, COLS)] = dq_rows[cols(h, PART), :]

    drain_core(CP + 5)
    rest_home(0)
    drain(acol.at[pl.ds(0, 62)], recv.at[A1])

    def arrange_out(number, carry):
        aperm[2 * number] = acol[owned[0, number]]
        aperm[2 * number + 1] = acol[owned[1, number]]
        return carry

    lax.fori_loop(0, N_CTX, arrange_out, 0, unroll=4)

    def deliver_out(step, carry):
        to = lax.rem(c + step, N_CTX)
        push(
            aperm.at[pl.ds(2 * to, 2)], ao.at[:, pl.ds(tile_row, 16), cols(tile_head, DIM)], A2, to, h
        )
        return carry

    lax.fori_loop(1, N_CTX, deliver_out, 0)
    own_out = pltpu.make_async_copy(
        aperm.at[pl.ds(2 * c, 2)], ao.at[:, pl.ds(tile_row, 16), cols(tile_head, DIM)], local.at[LA]
    )
    own_out.start()
    before_home(1)
    before_home(0)

    for which in (1, 0):
        drain(from_x.at[0, pl.ds(PLANES, 3)], recv.at[XPV + which])
        drain(from_x.at[0, 0], recv.at[XP + 3 * which])
        drain(from_x.at[0, 0, pl.ds(0, 3)], recv.at[XP + 3 * which + 2])
        drain(from_x.at[0, 0], recv.at[XP + 3 * which + 1])
        for head in range(N_HEAD):
            piece = from_x[which, 0, head].astype(F32)
            for number in range(1, PLANES + NY - 1):
                piece = piece + from_x[which, number, head].astype(F32)
            (gk, gv)[which][:, head * DIM : (head + 1) * DIM] = piece.astype(BF16)
    three_cols = pl.ds(0, 3 * COLS)
    drain(gperm.at[pl.ds(0, 62)], recv.at[A2])
    drain(gq.at[:, three_cols], recv.at[DQ])
    own_out.wait()
    for sem in (G1, G2, A1, A2):
        drain(gperm.at[pl.ds(0, 62)], send.at[sem])
    for sem in (XQ, DQ):
        drain(gq.at[:, three_cols], send.at[sem])
    for which in range(2):
        for sem in (X0 + which, XP + 3 * which + 2):
            drain(from_x.at[0, 0, pl.ds(0, 3)], send.at[sem])
        for sem in (X1 + which, X2 + which, XP + 3 * which, XP + 3 * which + 1):
            drain(from_x.at[0, 0], send.at[sem])
        for sem in (Y1, YV, YP, XPV):
            drain(from_y.at[0], send.at[sem + which])
        for sem in range(3):
            drain(from_y.at[0], send.at[CP + 3 * which + sem])
        drain(kv.at[0, pl.ds(0, NY), 0], send.at[C1 + which])
        drain(kv.at[0, pl.ds(0, NY + 1), 0], send.at[CV + which])


def finish_body(ao, gq, gk, gv, ao_out, gq_out, gk_out, gv_out, sems):
    copies = [
        pltpu.make_async_copy(src, dst, sems.at[number])
        for number, (src, dst) in enumerate(((ao, ao_out), (gq, gq_out), (gk, gk_out), (gv, gv_out)))
    ]
    for copy in copies:
        copy.start()
    for copy in copies:
        copy.wait()


def finish(*arrays):
    anywhere = pl.BlockSpec(memory_space=pltpu.VMEM)
    arrays = [pltpu.with_memory_space_constraint(array, pltpu.VMEM) for array in arrays]
    hbm = pl.BlockSpec(memory_space=pltpu.HBM)
    return pl.pallas_call(
        finish_body,
        out_shape=tuple(jax.ShapeDtypeStruct(array.shape, array.dtype) for array in arrays),
        in_specs=[anywhere] * 4,
        out_specs=(hbm,) * 4,
        scratch_shapes=[pltpu.SemaphoreType.DMA((4,))],
        name="write_outputs",
    )(*arrays)


def shards(queries, keys, values, grad_out, owner_lists, doc_lengths):
    hbm = pl.BlockSpec(memory_space=pltpu.HBM)
    smem = pl.BlockSpec(memory_space=pltpu.SMEM)
    block = (TOK, DIM)
    ao, gq, gk, gv = pl.pallas_call(
        body,
        out_shape=(
            pltpu.VMEM((2, TOK // 2, COLS), BF16),
            pltpu.VMEM((PART, N_HEAD * COLS), BF16),
            pltpu.VMEM((PART, N_HEAD * DIM), BF16),
            pltpu.VMEM((PART, N_HEAD * DIM), BF16),
        ),
        in_specs=[hbm] * 4 + [smem] * 2,
        out_specs=(pl.BlockSpec(memory_space=pltpu.VMEM),) * 4,
        scratch_shapes=[
            pltpu.VMEM((2, SLOTS, NCORE) + block, BF16),
            pltpu.VMEM((TOK, COLS), BF16),
            pltpu.VMEM((2 * N_CTX, 16, DIM), BF16),
            pltpu.VMEM((2 * N_CTX, 16, DIM), BF16),
            pltpu.VMEM((GROUP, 2, TOK // 2, DIM), BF16),
            pltpu.VMEM((2 * N_CTX, 16, DIM), BF16),
            pltpu.VMEM((2 * N_CTX, 16, DIM), BF16),
            pltpu.VMEM((GROUP, 2, TOK // 2, DIM), BF16),
            pltpu.VMEM((TOK, COLS), BF16),
            pltpu.VMEM((ROWS, DIM), BF16),
            pltpu.VMEM((DIM, ROWS), BF16),
            pltpu.VMEM((DIM, ROWS), BF16),
            pltpu.VMEM((SLOTS, PAIR, ROWS), F32),
            pltpu.VMEM((SLOTS, PAIR, ROWS), BF16),
            pltpu.VMEM((2, SLOTS, NCORE) + block, BF16),
            pltpu.VMEM((2, SLOTS) + block, BF16),
            pltpu.VMEM((2, NY - 1) + block, BF16),
            pltpu.VMEM((2, NY - 1) + block, BF16),
            pltpu.VMEM((2, PLANES + NY - 1) + block, BF16),
            pltpu.VMEM((2, PLANES + NY - 1, N_HEAD, PART, DIM), BF16),
            pltpu.VMEM((8, DIM), jnp.int32),
            pltpu.SMEM((8, DIM), jnp.int32),
            pltpu.SemaphoreType.DMA((N_SEM,)),
            pltpu.SemaphoreType.DMA((N_SEM,)),
            pltpu.SemaphoreType.DMA((N_LOCAL,)),
        ],
        compiler_params=pltpu.CompilerParams(
            collective_id=0, has_side_effects=True, vmem_limit_bytes=56 * 1024 * 1024
        ),
        cost_estimate=pl.CostEstimate(flops=4_000_000_000, bytes_accessed=4_000_000, transcendentals=2_300_000),
        name="attention_core",
    )(queries, keys, values, grad_out.reshape(2, TOK // 2, COLS), owner_lists.T, doc_lengths)
    return finish(ao.reshape(TOK, COLS), gq, gk, gv)


def solution(mesh):
    placed = (
        P(("ctx", "head"), None),
        P(("ctx", "head"), None),
        P(("ctx", "head"), None),
        P("ctx", "head"),
        P(),
        P(),
    )
    return jax.shard_map(
        shards,
        mesh=mesh,
        in_specs=placed,
        out_specs=(
            P("ctx", "head"),
            P(("ctx", "head"), None),
            P(("ctx", "head"), None),
            P(("ctx", "head"), None),
        ),
        check_vma=False,
    )
```
